512 devices in a mesh: tun: 128 (over z, x, core), hgt: 4 (over y).
Axes of the slice: x: 4, y: 4, z: 16, core: 2. Of those that a mesh axis runs over, the one named last changes fastest.
Arguments:
- cotangent: float32 [2, 512, 128, 256], P(None, 'tun', 'hgt'), may hold values from -16000 to 16000
- tun_cond: float32 [512, 128, 256], P('tun', 'hgt'), may hold values from 1024 to 2048
- tun_flow: float32 [512, 128, 256], P('tun', 'hgt'), may hold values from 32 to 64
- heat_loss: float32 [512, 128, 256], P('tun', 'hgt'), may hold values from 0.25 to 4
- hgt_cond: float32 [512, 128, 256], P('tun', 'hgt'), may hold values from 4096 to 16384
- hgt_lift: float32 [512, 128, 256], P('tun', 'hgt'), may hold values from 1024 to 4096
- wid_cond: float32 [257], replicated, may hold values from 0.25 to 1
Outputs:
- adjoint: float32 [2, 512, 128, 256], P(None, 'tun', 'hgt')
The draws below stay inside these ranges and needn't reach their ends.
All inputs are finite; a program needn't handle non-finite values.
Results may differ from the reference program's by a relative error of at most 0.0049.
Values sent between devices are 32-bit elements; how exact they have to be, the bound alone decides.
No kernel may reach another device: no remote copies, remote signals or barrier semaphores. Data moves between devices by JAX's collectives and lax.ppermute only.
A program may use at most 192 MiB of HBM per device.

```python
import math
import jax
import jax.numpy as jnp
from jax import lax

W = 256
NX = 512
NH = 128


def draw_cotangent(key, part):
    magnitude = 4000.0
    return magnitude * jax.random.truncated_normal(key, -4.0, 4.0, (2, NX, NH, W), jnp.float32)


def shard_levels(rng, dims, pieces, smallest, high):
    gain = 1.0
    for dim, blocks in pieces:
        heights = jax.random.uniform(jax.random.fold_in(jax.random.fold_in(rng, 6), dim), (blocks,), jnp.float32, smallest / len(pieces), high / len(pieces))
        gain = gain * jnp.repeat(jnp.exp(heights), dims[dim] // blocks).reshape((-1,) + (1,) * (len(dims) - 1 - dim))
    return gain


def setup_inputs(seed: int = 0) -> dict:
    splits = jax.random.split(jax.random.key(seed), 8)
    return {
        "cotangent": draw_cotangent(jax.random.fold_in(splits[7], 71), 0),
        "tun_cond": jnp.clip(jnp.exp(math.log(2048.0) - 0.6931472 * jax.random.uniform(splits[1], (NX, NH, W), jnp.float32) ** shard_levels(splits[1], (NX, NH, W), ((0, 128), (1, 4)), -0.2, 0.2)), 1024.0, 2048.0),
        "tun_flow": jnp.clip(jnp.exp(math.log(64.0) - 0.6931472 * jax.random.uniform(splits[2], (NX, NH, W), jnp.float32) ** shard_levels(splits[2], (NX, NH, W), ((0, 128), (1, 4)), -0.2, 0.2)), 32.0, 64.0),
        "heat_loss": jnp.clip(jnp.exp(math.log(4.0) - 2.7725887 * jax.random.uniform(splits[3], (NX, NH, W), jnp.float32) ** shard_levels(splits[3], (NX, NH, W), ((0, 128), (1, 4)), -0.2, 0.2)), 0.25, 4.0),
        "hgt_cond": jnp.clip(jnp.exp(math.log(16384.0) - 1.3862944 * jax.random.uniform(splits[4], (NX, NH, W), jnp.float32) ** shard_levels(splits[4], (NX, NH, W), ((0, 128), (1, 4)), -0.2, 0.2)), 4096.0, 16384.0),
        "hgt_lift": jnp.clip(jnp.exp(math.log(4096.0) - 1.3862944 * jax.random.uniform(splits[5], (NX, NH, W), jnp.float32) ** shard_levels(splits[5], (NX, NH, W), ((0, 128), (1, 4)), -0.2, 0.2)), 1024.0, 4096.0),
        "wid_cond": jnp.clip(jnp.exp(jax.random.uniform(splits[6], (W + 1,), jnp.float32, math.log(0.25), math.log(1.0))), 0.25, 1.0),
    }


def thomas_sweep(sub_diag, main_diag, super_diag, source):

    def forward(carry, packed):
        prior_pivot, prior_reduced = carry
        sub_row, main_row, super_row, source_row = packed
        denominator = main_row - sub_row * prior_pivot
        pivot_now = super_row / denominator
        reduced_now = (source_row - sub_row * prior_reduced) / denominator
        return ((pivot_now, reduced_now), (pivot_now, reduced_now))
    anchor = jnp.zeros_like(source[0])
    unused, (pivots, reduced_all) = lax.scan(forward, (anchor, anchor), (sub_diag, main_diag, super_diag, source))

    def backward(following, packed):
        pivot_now, reduced_now = packed
        solved = reduced_now - pivot_now * following
        return (solved, solved)
    unused_back, solution = lax.scan(backward, anchor, (pivots, reduced_all), reverse=True)
    return solution

def transposed_solve(conduct, flow_face, added_diag, source):
    cond_next = jnp.concatenate([conduct[1:], jnp.zeros_like(conduct[:1])], axis=0)
    flow_next = jnp.concatenate([flow_face[1:], jnp.zeros_like(flow_face[:1])], axis=0)
    main_diag = 1.0 + added_diag + conduct + cond_next + flow_next
    return thomas_sweep(-conduct, main_diag, -(cond_next + flow_next), source)

def reference(cotangent, tun_cond, tun_flow, heat_loss, hgt_cond, hgt_lift, wid_cond):
    moved = jnp.moveaxis(cotangent, 2, 0)
    cond_up = jnp.moveaxis(hgt_cond, 1, 0)[:, None]
    lift_up = jnp.moveaxis(hgt_lift, 1, 0)[:, None]
    lifted = jnp.moveaxis(transposed_solve(cond_up, lift_up, 0.0, moved), 0, 2)
    moved = jnp.moveaxis(lifted, 1, 0)
    energy_loss = jnp.stack([heat_loss, jnp.zeros_like(heat_loss)], axis=1)
    carried = jnp.moveaxis(transposed_solve(tun_cond[:, None], tun_flow[:, None], energy_loss, moved), 0, 1)
    width_cells = wid_cond.shape[0] - 1
    main_width = 1.0 + wid_cond[:-1] + wid_cond[1:]
    off_width = -wid_cond[1:-1]
    matrix = jnp.diag(main_width) + jnp.diag(off_width, 1) + jnp.diag(off_width, -1)
    flat = carried.reshape(-1, width_cells)
    solved = jnp.linalg.solve(matrix, flat.T).T
    return solved.reshape(carried.shape)
```

```python
import jax
import jax.numpy as jnp
from jax import lax
from jax.experimental import pallas as pl
from jax.experimental.pallas import tpu as pltpu
from jax.sharding import PartitionSpec as P

F32 = jnp.float32
LANES = 128


def vmem(count):
    return [pl.BlockSpec(memory_space=pltpu.VMEM)] * count


def joined(element, following):
    up, mp, low, m, rp, r = element
    next_up, next_mp, next_low, next_m, next_rp, next_r = following
    mid = m + next_mp
    inverse = 1.0 / (mid + low + next_up)
    a, b, mid = low * inverse, next_up * inverse, mid * inverse
    c = [(one + two) * inverse for one, two in zip(r, next_rp)]
    whole = (
        up * b,
        mp + up * mid,
        next_low * a,
        next_m + next_low * mid,
        [one + up * two for one, two in zip(rp, c)],
        [one + next_low * two for one, two in zip(next_r, c)],
    )
    return whole, a, b, c


def height_forward(field, cond, lift, elements, saved, middle, pieces, fields, conds, lifts):
    lower = [pl.ds(0, 4, stride=2), pl.ds(1, 4, stride=2)]
    for half in range(2):
        lanes = pl.ds(half * LANES, LANES)

        fields[half], conds[half], lifts[half] = field[:, lanes], cond[:, lanes], lift[:, lanes]

        def cell(ref, index, base=0):
            return ref[half, pl.ds(base + index, 8, stride=16), :]

        def one(index):
            k = cell(conds, index)
            return (
                k + cell(lifts, index),
                jnp.zeros_like(k),
                k,
                jnp.ones_like(k),
                [jnp.zeros_like(k)] * 2,
                [cell(fields, index), cell(fields, index, 128)],
            )

        element = one(0)
        for index in range(1, 16):
            element, a, b, c = joined(element, one(index))
            for place, part in enumerate((a, b, *c)):
                saved[place, index - 1, :, lanes] = part
        up, mp, low, m, rp, r = element
        for place, part in enumerate((up, mp, low, m, *rp, *r)):
            pieces[half, place] = part

        def sub(which):
            up, mp, low, m, rp0, rp1, r0, r1 = (pieces[half, place, lower[which]] for place in range(8))
            return up, mp, low, m, [rp0, rp1], [r0, r1]

        whole, a, b, c = joined(sub(0), sub(1))
        for place, part in enumerate((a, b, *c)):
            middle[pl.ds(4 * place, 4), lanes] = part
        up, mp, low, m, rp, r = whole
        for place, part in enumerate((up, mp, low, m, *rp, *r)):
            for target in range(4):
                elements[target, pl.ds(4 * place, 4), lanes] = part


def height_back(elements, saved, middle, cond, flow, loss, sent, kept, bound, ends, lifted):
    def part(source, place, rows=4):
        return elements[source, pl.ds(4 * place, rows), :]

    rows_of = []
    for source in range(4):
        low, m, r = part(source, 2), part(source, 3), part(source, 6, 8)
        if source == 0:
            low, m = jnp.zeros_like(low), m + low
        up = jnp.zeros_like(low)
        if source < 3:
            up, m, r = part(source + 1, 0), m + part(source + 1, 1), r + part(source + 1, 4, 8)
        rows_of.append([low, m, up, r])

    def twice(value):
        return jnp.concatenate([value, value], axis=0)

    scale = []
    for source in range(4):
        low, m, up, r = rows_of[source]
        inverse = 1.0 / (m + up)
        scale.append((twice(up * inverse), r * twice(inverse)))
        if source < 3:
            after = rows_of[source + 1]
            after[1] = after[1] + after[0] * (m * inverse)
            after[3] = after[3] + twice(after[0]) * scale[source][1]
    bound[0] = jnp.zeros_like(bound[0])
    value = scale[3][1]
    bound[4] = value
    for source in (2, 1, 0):
        value = scale[source][1] + scale[source][0] * value
        bound[source + 1] = value
    mine = lax.axis_index("hgt")
    before, last = bound[mine], bound[mine + 1]
    a, b, c = middle[0:4, :], middle[4:8, :], middle[8:16, :]
    centre = c + twice(a) * before + twice(b) * last
    even, odd = pl.ds(0, 4, stride=2), pl.ds(1, 4, stride=2)
    for half in range(2):
        lanes = pl.ds(half * LANES, LANES)
        cut = slice(half * LANES, (half + 1) * LANES)
        for comp in range(2):
            rows = slice(4 * comp, 4 * comp + 4)
            ends[half, comp, 0, even] = before[rows, cut]
            ends[half, comp, 0, odd] = centre[rows, cut]
            ends[half, comp, 1, even] = centre[rows, cut]
            ends[half, comp, 1, odd] = last[rows, cut]
            start, value = ends[half, comp, 0], ends[half, comp, 1]
            lifted[half, pl.ds(128 * comp + 15, 8, stride=16), :] = value
            for index in range(14, -1, -1):
                value = (
                    saved[2 + comp, index, :, lanes]
                    + saved[0, index, :, lanes] * start
                    + saved[1, index, :, lanes] * value
                )
                lifted[half, pl.ds(128 * comp + index, 8, stride=16), :] = value
    for block in range(4):
        for half in range(2):
            lanes = pl.ds(half * LANES, LANES)
            for comp in range(2):

                def one(index):
                    rows = pl.ds(32 * index + 8 * block, 8)
                    k = cond[rows, lanes]
                    m = 1.0 + loss[rows, lanes] if comp == 0 else jnp.ones_like(k)
                    r = lifted[half, pl.ds(128 * comp + 32 * index + 8 * block, 8), :]
                    zero = jnp.zeros_like(k)
                    return k + flow[rows, lanes], zero, k, m, [zero], [r]

                element = one(0)
                for index in range(1, 4):
                    element, a, b, c = joined(element, one(index))
                    for place, value in enumerate((a, b, *c)):
                        kept[4 * comp + block, index - 1, place, :, lanes] = value
                up, mp, low, m, rp, r = element
                for place, value in enumerate((up, mp, low, m, *rp, *r)):
                    sent[4 * comp + block, place, :, lanes] = value


def chain_forward(received, sent, kept):
    def one(index):
        up, mp, low, m, rp, r = (received[index, place] for place in range(6))
        return up, mp, low, m, [rp], [r]

    element = one(0)
    for index in range(1, 8):
        element, a, b, c = joined(element, one(index))
        for place, value in enumerate((a, b, *c)):
            kept[index - 1, place] = value
    up, mp, low, m, rp, r = element
    for place, value in enumerate((up, mp, low, m, *rp, *r, *r, *r)):
        for half in range(2):
            sent[pl.ds(8 * half + place, 8, stride=16), :] = value[:, half * LANES : (half + 1) * LANES]


def chain_solve(received, sent):
    count = 16
    up, mp, low, m, rp, r = (received[pl.ds(place, count, stride=8), :] for place in range(6))

    def earlier(value, step):
        return jnp.concatenate([jnp.zeros_like(value[:step]), value[:-step]], axis=0)

    def later(value, step):
        return jnp.concatenate([value[step:], jnp.zeros_like(value[:step])], axis=0)

    first = lax.broadcasted_iota(jnp.int32, low.shape, 0) == 0
    m = m + later(mp, 1) + jnp.where(first, low, 0.0)
    low = jnp.where(first, 0.0, low)
    up, r = later(up, 1), r + later(rp, 1)
    step = 1
    while step < count:
        inverse = 1.0 / (low + m + up)
        part, right = m * inverse, r * inverse
        m, r, low, up = (
            m + low * earlier(part, step) + up * later(part, step),
            r + low * earlier(right, step) + up * later(right, step),
            low * earlier(low * inverse, step),
            up * later(up * inverse, step),
        )
        step *= 2
    value = r / m
    sent[pl.ds(0, count, stride=2), :] = earlier(value, 1)
    sent[pl.ds(1, count, stride=2), :] = value


def chain_back(received, kept, sent):
    def end(which):
        return jnp.concatenate([received[pl.ds(2 * half + which, 8, stride=4), :] for half in range(2)], axis=1)

    before, value = end(0), end(1)
    sent[7, 1] = value
    for index in range(6, -1, -1):
        value = kept[index, 2] + kept[index, 0] * before + kept[index, 1] * value
        sent[index, 1] = value
        sent[index + 1, 0] = value
    sent[0, 0] = before


def split(value):
    high = value.astype(jnp.bfloat16)
    return high, (value - high.astype(F32)).astype(jnp.bfloat16)


def tunnel_back(received, kept, high, low, out, carried):
    for group in range(8):
        comp, block = group // 4, group % 4
        before, value = received[group, 0], received[group, 1]
        for index in range(3, -1, -1):
            if index < 3:
                value = kept[group, index, 2] + kept[group, index, 0] * before + kept[group, index, 1] * value
            carried[pl.ds(128 * comp + 32 * index + 8 * block, 8), :] = value
    top, rest = split(carried[...])

    def times(one, two):
        return jnp.dot(one, two[...], preferred_element_type=F32)

    out[...] = times(top, high) + (times(top, low) + times(rest, high))


def width_inverse(below, above, high, low_part):
    count = 256
    step = 1
    lower, upper = below[...], above[...]
    row = lax.broadcasted_iota(jnp.int32, (count, LANES), 0)
    one = jnp.ones((count, LANES), F32)
    m = one + jnp.where(row == 0, lower, 0.0) + jnp.where(row == count - 1, upper, 0.0)
    low, up = jnp.where(row == 0, 0.0, lower), jnp.where(row == count - 1, 0.0, upper)
    column = lax.broadcasted_iota(jnp.int32, (count, LANES), 1)
    rights = [jnp.where(row == column + LANES * half, 1.0, 0.0) for half in range(2)]

    def earlier(value, step):
        return jnp.concatenate([jnp.zeros_like(value[:step]), value[:-step]], axis=0)

    def later(value, step):
        return jnp.concatenate([value[step:], jnp.zeros_like(value[:step])], axis=0)

    while step < count:
        inverse = 1.0 / (low + m + up)
        part = m * inverse
        scaled = [right * inverse for right in rights]
        rights = [
            right + low * earlier(value, step) + up * later(value, step) for right, value in zip(rights, scaled)
        ]
        m, low, up = (
            m + low * earlier(part, step) + up * later(part, step),
            low * earlier(low * inverse, step),
            up * later(up * inverse, step),
        )
        step *= 2
    for half in range(2):
        lanes = pl.ds(half * LANES, LANES)
        top, rest = split(rights[half] / m)
        high[:, lanes] = top
        low_part[:, lanes] = rest


def call(kernel, outs, scratch, *args):
    result = pl.pallas_call(
        kernel,
        out_shape=[jax.ShapeDtypeStruct(shape, dtype) for shape, dtype in outs],
        in_specs=vmem(len(args)),
        out_specs=vmem(len(outs)),
        scratch_shapes=[pltpu.VMEM(shape, F32) for shape in scratch],
        compiler_params=pltpu.CompilerParams(vmem_limit_bytes=16 * 2**20),
    )(*args)
    return result


def per_device(cotangent, tun_cond, tun_flow, heat_loss, hgt_cond, hgt_lift, wid_cond):
    near = [[8 * z + other for other in range(8)] for z in range(16)]
    far = [[8 * z + other for z in range(16)] for other in range(8)]

    def exchanged(value, axis, groups=None):
        return lax.all_to_all(value, axis, 0, 0, tiled=True, axis_index_groups=groups)

    def rows(value):
        return value.reshape(-1, 256)

    lower = jnp.broadcast_to(wid_cond[:256, None], (256, LANES))
    upper = jnp.broadcast_to(wid_cond[1:, None], (256, LANES))
    high, low = call(width_inverse, [((256, 256), jnp.bfloat16)] * 2, [], lower, upper)

    elements, saved, middle = call(
        height_forward,
        [((4, 32, 256), F32), ((4, 15, 8, 256), F32), ((16, 256), F32)],
        [(2, 8, 8, LANES), (2, 256, LANES), (2, 128, LANES), (2, 128, LANES)],
        rows(cotangent),
        rows(hgt_cond),
        rows(hgt_lift),
    )
    elements = exchanged(elements, "hgt")
    sent, kept = call(
        height_back,
        [((8, 6, 8, 256), F32), ((8, 3, 3, 8, 256), F32)],
        [(5, 8, 256), (2, 2, 2, 8, LANES), (2, 256, LANES)],
        elements,
        saved,
        middle,
        rows(tun_cond),
        rows(tun_flow),
        rows(heat_loss),
    )
    received = exchanged(sent, "tun", near)
    sent, chain = call(chain_forward, [((128, LANES), F32), ((7, 3, 8, 256), F32)], [], received)
    received = exchanged(sent.reshape(16, 8, LANES), "tun", far).reshape(128, LANES)
    [sent] = call(chain_solve, [((32, LANES), F32)], [], received)
    received = exchanged(sent.reshape(16, 2, LANES), "tun", far).reshape(32, LANES)
    [sent] = call(chain_back, [((8, 2, 8, 256), F32)], [], received, chain)
    received = exchanged(sent, "tun", near)
    [solved] = call(tunnel_back, [((256, 256), F32)], [(256, 256)], received, kept, high, low)
    return solved.reshape(cotangent.shape)


def solution(mesh):
    in_specs = (
        P(None, "tun", "hgt", None),
        P("tun", "hgt", None),
        P("tun", "hgt", None),
        P("tun", "hgt", None),
        P("tun", "hgt", None),
        P("tun", "hgt", None),
        P(),
    )
    out_specs = P(None, "tun", "hgt", None)
    return jax.shard_map(
        per_device, mesh=mesh, in_specs=in_specs, out_specs=out_specs, check_vma=False
    )
```

```python
import jax
import jax.numpy as jnp
from jax import lax
from jax.experimental import pallas as pl
from jax.experimental.pallas import tpu as pltpu
from jax.sharding import PartitionSpec as P

F32 = jnp.float32
LANES = 128


def vmem(count):
    return [pl.BlockSpec(memory_space=pltpu.VMEM)] * count


def joined(element, following):
    up, mp, low, m, rp, r = element
    next_up, next_mp, next_low, next_m, next_rp, next_r = following
    mid = m + next_mp
    inverse = 1.0 / (mid + low + next_up)
    a, b, mid = low * inverse, next_up * inverse, mid * inverse
    c = [(one + two) * inverse for one, two in zip(r, next_rp)]
    whole = (
        up * b,
        mp + up * mid,
        next_low * a,
        next_m + next_low * mid,
        [one + up * two for one, two in zip(rp, c)],
        [one + next_low * two for one, two in zip(next_r, c)],
    )
    return whole, a, b, c


def height_forward(field, cond, lift, elements, saved, middle, pieces, fields, conds, lifts):
    lower = [pl.ds(0, 4, stride=2), pl.ds(1, 4, stride=2)]
    for half in range(2):
        lanes = pl.ds(half * LANES, LANES)

        fields[half], conds[half], lifts[half] = field[:, lanes], cond[:, lanes], lift[:, lanes]

        def cell(ref, index, base=0):
            return ref[half, pl.ds(base + index, 8, stride=16), :]

        def one(index):
            k = cell(conds, index)
            return (
                k + cell(lifts, index),
                jnp.zeros_like(k),
                k,
                jnp.ones_like(k),
                [jnp.zeros_like(k)] * 2,
                [cell(fields, index), cell(fields, index, 128)],
            )

        element = one(0)
        for index in range(1, 16):
            element, a, b, c = joined(element, one(index))
            for place, part in enumerate((a, b, *c)):
                saved[place, index - 1, :, lanes] = part
        up, mp, low, m, rp, r = element
        for place, part in enumerate((up, mp, low, m, *rp, *r)):
            pieces[half, place] = part

        def sub(which):
            up, mp, low, m, rp0, rp1, r0, r1 = (pieces[half, place, lower[which]] for place in range(8))
            return up, mp, low, m, [rp0, rp1], [r0, r1]

        whole, a, b, c = joined(sub(0), sub(1))
        for place, part in enumerate((a, b, *c)):
            middle[pl.ds(4 * place, 4), lanes] = part
        up, mp, low, m, rp, r = whole
        for place, part in enumerate((up, mp, low, m, *rp, *r)):
            for target in range(4):
                elements[target, pl.ds(4 * place, 4), lanes] = part


def height_back(elements, saved, middle, cond, flow, loss, sent, kept, bound, ends, lifted):
    def part(source, place, rows=4):
        return elements[source, pl.ds(4 * place, rows), :]

    rows_of = []
    for source in range(4):
        low, m, r = part(source, 2), part(source, 3), part(source, 6, 8)
        if source == 0:
            low, m = jnp.zeros_like(low), m + low
        up = jnp.zeros_like(low)
        if source < 3:
            up, m, r = part(source + 1, 0), m + part(source + 1, 1), r + part(source + 1, 4, 8)
        rows_of.append([low, m, up, r])

    def twice(value):
        return jnp.concatenate([value, value], axis=0)

    scale = []
    for source in range(4):
        low, m, up, r = rows_of[source]
        inverse = 1.0 / (m + up)
        scale.append((twice(up * inverse), r * twice(inverse)))
        if source < 3:
            after = rows_of[source + 1]
            after[1] = after[1] + after[0] * (m * inverse)
            after[3] = after[3] + twice(after[0]) * scale[source][1]
    bound[0] = jnp.zeros_like(bound[0])
    value = scale[3][1]
    bound[4] = value
    for source in (2, 1, 0):
        value = scale[source][1] + scale[source][0] * value
        bound[source + 1] = value
    mine = lax.axis_index("hgt")
    before, last = bound[mine], bound[mine + 1]
    a, b, c = middle[0:4, :], middle[4:8, :], middle[8:16, :]
    centre = c + twice(a) * before + twice(b) * last
    even, odd = pl.ds(0, 4, stride=2), pl.ds(1, 4, stride=2)
    for half in range(2):
        lanes = pl.ds(half * LANES, LANES)
        cut = slice(half * LANES, (half + 1) * LANES)
        for comp in range(2):
            rows = slice(4 * comp, 4 * comp + 4)
            ends[half, comp, 0, even] = before[rows, cut]
            ends[half, comp, 0, odd] = centre[rows, cut]
            ends[half, comp, 1, even] = centre[rows, cut]
            ends[half, comp, 1, odd] = last[rows, cut]
            start, value = ends[half, comp, 0], ends[half, comp, 1]
            lifted[half, pl.ds(128 * comp + 15, 8, stride=16), :] = value
            for index in range(14, -1, -1):
                value = (
                    saved[2 + comp, index, :, lanes]
                    + saved[0, index, :, lanes] * start
                    + saved[1, index, :, lanes] * value
                )
                lifted[half, pl.ds(128 * comp + index, 8, stride=16), :] = value
    for block in range(4):
        for half in range(2):
            lanes = pl.ds(half * LANES, LANES)
            for comp in range(2):

                def one(index):
                    rows = pl.ds(32 * index + 8 * block, 8)
                    k = cond[rows, lanes]
                    m = 1.0 + loss[rows, lanes] if comp == 0 else jnp.ones_like(k)
                    r = lifted[half, pl.ds(128 * comp + 32 * index + 8 * block, 8), :]
                    zero = jnp.zeros_like(k)
                    return k + flow[rows, lanes], zero, k, m, [zero], [r]

                element = one(0)
                for index in range(1, 4):
                    element, a, b, c = joined(element, one(index))
                    for place, value in enumerate((a, b, *c)):
                        kept[4 * comp + block, index - 1, place, :, lanes] = value
                up, mp, low, m, rp, r = element
                for place, value in enumerate((up, mp, low, m, *rp, *r)):
                    sent[2 * (4 * comp + block) + half, place] = value


def tree(elements, first, last, keep):
    if last - first == 1:
        return elements(first)
    centre = (first + last) // 2
    left, right = tree(elements, first, centre, keep), tree(elements, centre, last, keep)
    whole, a, b, c = joined(left, right)
    keep(centre - 1, a, b, c)
    return whole


def untree(kept, first, last, before, value, give):
    if last - first == 1:
        return
    centre = (first + last) // 2
    a, b, c = kept(centre - 1)
    middle = c + a * before + b * value
    give(centre - 1, middle)
    untree(kept, first, centre, before, middle, give)
    untree(kept, centre, last, middle, value, give)


def chain_forward(received, sent, kept):
    def one(index):
        up, mp, low, m, rp, r = (received[index, place] for place in range(6))
        return up, mp, low, m, [rp], [r]

    def keep(index, a, b, c):
        kept[index, 0], kept[index, 1], kept[index, 2] = a, b, c[0]

    up, mp, low, m, rp, r = tree(one, 0, received.shape[0], keep)
    for place, value in enumerate((up, mp, low, m, *rp, *r)):
        for target in range(sent.shape[0]):
            sent[target, place] = value


def chain_back(received, kept, sent, bound):
    groups, members = received.shape[0], sent.shape[0]
    top = {}

    def one(index):
        up, mp, low, m, rp, r = (received[index, place] for place in range(6))
        return up, mp, low, m, [rp], [r]

    def keep(index, a, b, c):
        top[index] = a, b, c[0]

    def give(index, value):
        bound[index + 1] = value

    up, mp, low, m, rp, r = tree(one, 0, groups, keep)
    zero = jnp.zeros_like(up)
    value = r[0] / (low + m)
    bound[0] = zero
    give(groups - 1, value)
    untree(lambda index: top[index], 0, groups, zero, value, give)
    mine = lax.axis_index("tun") // members
    before, value = bound[mine], bound[mine + 1]

    def end(index, value):
        sent[index, 1] = value
        if index + 1 < members:
            sent[index + 1, 0] = value

    sent[0, 0] = before
    end(members - 1, value)
    untree(lambda index: [kept[index, place] for place in range(3)], 0, members, before, value, end)


def split(value):
    high = value.astype(jnp.bfloat16)
    return high, (value - high.astype(F32)).astype(jnp.bfloat16)


def tunnel_back(received, kept, high, low, out, carried):
    for group in range(8):
        comp, block = group // 4, group % 4
        for half in range(2):
            lanes = pl.ds(half * LANES, LANES)
            before, value = received[2 * group + half, 0], received[2 * group + half, 1]
            for index in range(3, -1, -1):
                if index < 3:
                    a, b, c = (kept[group, index, place, :, lanes] for place in range(3))
                    value = c + a * before + b * value
                carried[pl.ds(128 * comp + 32 * index + 8 * block, 8), lanes] = value
    top, rest = split(carried[...])

    def times(one, two):
        return jnp.dot(one, two[...], preferred_element_type=F32)

    out[...] = times(top, high) + (times(top, low) + times(rest, high))


def width_inverse(below, above, high, low_part):
    count = 256
    step = 1
    lower, upper = below[...], above[...]
    row = lax.broadcasted_iota(jnp.int32, (count, LANES), 0)
    one = jnp.ones((count, LANES), F32)
    m = one + jnp.where(row == 0, lower, 0.0) + jnp.where(row == count - 1, upper, 0.0)
    low, up = jnp.where(row == 0, 0.0, lower), jnp.where(row == count - 1, 0.0, upper)
    column = lax.broadcasted_iota(jnp.int32, (count, LANES), 1)
    rights = [jnp.where(row == column + LANES * half, 1.0, 0.0) for half in range(2)]

    def earlier(value, step):
        return jnp.concatenate([jnp.zeros_like(value[:step]), value[:-step]], axis=0)

    def later(value, step):
        return jnp.concatenate([value[step:], jnp.zeros_like(value[:step])], axis=0)

    while step < count:
        inverse = 1.0 / (low + m + up)
        part = m * inverse
        scaled = [right * inverse for right in rights]
        rights = [
            right + low * earlier(value, step) + up * later(value, step) for right, value in zip(rights, scaled)
        ]
        m, low, up = (
            m + low * earlier(part, step) + up * later(part, step),
            low * earlier(low * inverse, step),
            up * later(up * inverse, step),
        )
        step *= 2
    for half in range(2):
        lanes = pl.ds(half * LANES, LANES)
        top, rest = split(rights[half] / m)
        high[:, lanes] = top
        low_part[:, lanes] = rest


def call(kernel, outs, scratch, *args):
    result = pl.pallas_call(
        kernel,
        out_shape=[jax.ShapeDtypeStruct(shape, dtype) for shape, dtype in outs],
        in_specs=vmem(len(args)),
        out_specs=vmem(len(outs)),
        scratch_shapes=[pltpu.VMEM(shape, F32) for shape in scratch],
        compiler_params=pltpu.CompilerParams(vmem_limit_bytes=16 * 2**20),
    )(*args)
    return result


def per_device(cotangent, tun_cond, tun_flow, heat_loss, hgt_cond, hgt_lift, wid_cond):
    members = 16
    count = lax.axis_size("tun")
    near = [list(range(first, first + members)) for first in range(0, count, members)]
    far = [list(range(first, count, members)) for first in range(members)]
    groups = len(near)

    def exchanged(value, axis, groups=None):
        return lax.all_to_all(value, axis, 0, 0, tiled=True, axis_index_groups=groups)

    def rows(value):
        return value.reshape(-1, 256)

    lower = jnp.broadcast_to(wid_cond[:256, None], (256, LANES))
    upper = jnp.broadcast_to(wid_cond[1:, None], (256, LANES))
    high, low = call(width_inverse, [((256, 256), jnp.bfloat16)] * 2, [], lower, upper)

    elements, saved, middle = call(
        height_forward,
        [((4, 32, 256), F32), ((4, 15, 8, 256), F32), ((16, 256), F32)],
        [(2, 8, 8, LANES), (2, 256, LANES), (2, 128, LANES), (2, 128, LANES)],
        rows(cotangent),
        rows(hgt_cond),
        rows(hgt_lift),
    )
    elements = exchanged(elements, "hgt")
    sent, kept = call(
        height_back,
        [((members, 6, 8, LANES), F32), ((8, 3, 3, 8, 256), F32)],
        [(5, 8, 256), (2, 2, 2, 8, LANES), (2, 256, LANES)],
        elements,
        saved,
        middle,
        rows(tun_cond),
        rows(tun_flow),
        rows(heat_loss),
    )
    received = exchanged(sent, "tun", near)
    sent, chain = call(
        chain_forward, [((groups, 6, 8, LANES), F32), ((members - 1, 3, 8, LANES), F32)], [], received
    )
    received = exchanged(sent, "tun", far)
    [sent] = call(
        chain_back, [((members, 2, 8, LANES), F32)], [(groups + 1, 8, LANES)], received, chain
    )
    received = exchanged(sent, "tun", near)
    [solved] = call(tunnel_back, [((256, 256), F32)], [(256, 256)], received, kept, high, low)
    return solved.reshape(cotangent.shape)


def solution(mesh):
    in_specs = (
        P(None, "tun", "hgt", None),
        P("tun", "hgt", None),
        P("tun", "hgt", None),
        P("tun", "hgt", None),
        P("tun", "hgt", None),
        P("tun", "hgt", None),
        P(),
    )
    out_specs = P(None, "tun", "hgt", None)
    return jax.shard_map(
        per_device, mesh=mesh, in_specs=in_specs, out_specs=out_specs, check_vma=False
    )
```

```python
import jax
import jax.numpy as jnp
from jax import lax
from jax.experimental import pallas as pl
from jax.experimental.pallas import tpu as pltpu
from jax.sharding import PartitionSpec as P

F32 = jnp.float32
LANES = 128


def joined(element, following):
    up, mp, low, m, rp, r = element
    next_up, next_mp, next_low, next_m, next_rp, next_r = following
    mid = m + next_mp
    inverse = 1.0 / (mid + low + next_up)
    a, b, mid = low * inverse, next_up * inverse, mid * inverse
    c = [(one + two) * inverse for one, two in zip(r, next_rp)]
    whole = (
        up * b,
        mp + up * mid,
        next_low * a,
        next_m + next_low * mid,
        [one + up * two for one, two in zip(rp, c)],
        [one + next_low * two for one, two in zip(next_r, c)],
    )
    return whole, a, b, c


def front(field, cond, lift, wide, elements, saved, middle, high, rest, pieces, fields, conds, lifts, face, done):
    face_copy = pltpu.make_async_copy(wide, face, done.at[6])
    face_copy.start()
    copies = []
    for source, target in ((field, fields), (cond, conds), (lift, lifts)):
        for half in range(2):
            copy = pltpu.make_async_copy(
                source.at[:, pl.ds(half * LANES, LANES)], target.at[half], done.at[len(copies)]
            )
            copy.start()
            copies.append(copy)
    face_copy.wait()
    width_inverse(face, high, rest)
    for copy in copies:
        copy.wait()
    height_forward(elements, saved, middle, pieces, fields, conds, lifts)


def height_forward(elements, saved, middle, pieces, fields, conds, lifts):
    lower = [pl.ds(0, 4, stride=2), pl.ds(1, 4, stride=2)]
    for half in range(2):
        lanes = pl.ds(half * LANES, LANES)


        def cell(ref, index, base=0):
            return ref[half, pl.ds(base + index, 8, stride=16), :]

        def one(index):
            k = cell(conds, index)
            return (
                k + cell(lifts, index),
                jnp.zeros_like(k),
                k,
                jnp.ones_like(k),
                [jnp.zeros_like(k)] * 2,
                [cell(fields, index), cell(fields, index, 128)],
            )

        element = one(0)
        for index in range(1, 16):
            element, a, b, c = joined(element, one(index))
            for place, part in enumerate((a, b, *c)):
                saved[place, index - 1, :, lanes] = part
        up, mp, low, m, rp, r = element
        for place, part in enumerate((up, mp, low, m, *rp, *r)):
            pieces[half, place] = part

        def sub(which):
            up, mp, low, m, rp0, rp1, r0, r1 = (pieces[half, place, lower[which]] for place in range(8))
            return up, mp, low, m, [rp0, rp1], [r0, r1]

        whole, a, b, c = joined(sub(0), sub(1))
        for place, part in enumerate((a, b, *c)):
            middle[pl.ds(4 * place, 4), lanes] = part
        up, mp, low, m, rp, r = whole
        for place, part in enumerate((up, mp, low, m, *rp, *r)):
            for target in range(4):
                elements[target, pl.ds(4 * place, 4), lanes] = part


def height_back(elements, saved, middle, cond, flow, loss, sent, kept, bound, ends, lifted):
    def part(source, place, rows=4):
        return elements[source, pl.ds(4 * place, rows), :]

    rows_of = []
    for source in range(4):
        low, m, r = part(source, 2), part(source, 3), part(source, 6, 8)
        if source == 0:
            low, m = jnp.zeros_like(low), m + low
        up = jnp.zeros_like(low)
        if source < 3:
            up, m, r = part(source + 1, 0), m + part(source + 1, 1), r + part(source + 1, 4, 8)
        rows_of.append([low, m, up, r])

    def twice(value):
        return jnp.concatenate([value, value], axis=0)

    scale = []
    for source in range(4):
        low, m, up, r = rows_of[source]
        inverse = 1.0 / (m + up)
        scale.append((twice(up * inverse), r * twice(inverse)))
        if source < 3:
            after = rows_of[source + 1]
            after[1] = after[1] + after[0] * (m * inverse)
            after[3] = after[3] + twice(after[0]) * scale[source][1]
    bound[0] = jnp.zeros_like(bound[0])
    value = scale[3][1]
    bound[4] = value
    for source in (2, 1, 0):
        value = scale[source][1] + scale[source][0] * value
        bound[source + 1] = value
    mine = lax.axis_index("hgt")
    before, last = bound[mine], bound[mine + 1]
    a, b, c = middle[0:4, :], middle[4:8, :], middle[8:16, :]
    centre = c + twice(a) * before + twice(b) * last
    even, odd = pl.ds(0, 4, stride=2), pl.ds(1, 4, stride=2)
    for half in range(2):
        lanes = pl.ds(half * LANES, LANES)
        cut = slice(half * LANES, (half + 1) * LANES)
        for comp in range(2):
            rows = slice(4 * comp, 4 * comp + 4)
            ends[half, comp, 0, even] = before[rows, cut]
            ends[half, comp, 0, odd] = centre[rows, cut]
            ends[half, comp, 1, even] = centre[rows, cut]
            ends[half, comp, 1, odd] = last[rows, cut]
            start, value = ends[half, comp, 0], ends[half, comp, 1]
            lifted[half, pl.ds(128 * comp + 15, 8, stride=16), :] = value
            for index in range(14, -1, -1):
                value = (
                    saved[2 + comp, index, :, lanes]
                    + saved[0, index, :, lanes] * start
                    + saved[1, index, :, lanes] * value
                )
                lifted[half, pl.ds(128 * comp + index, 8, stride=16), :] = value
    for block in range(4):
        for half in range(2):
            lanes = pl.ds(half * LANES, LANES)
            for comp in range(2):

                def one(index):
                    rows = pl.ds(32 * index + 8 * block, 8)
                    k = cond[rows, lanes]
                    m = 1.0 + loss[rows, lanes] if comp == 0 else jnp.ones_like(k)
                    r = lifted[half, pl.ds(128 * comp + 32 * index + 8 * block, 8), :]
                    zero = jnp.zeros_like(k)
                    return k + flow[rows, lanes], zero, k, m, [zero], [r]

                element = one(0)
                for index in range(1, 4):
                    element, a, b, c = joined(element, one(index))
                    for place, value in enumerate((a, b, *c)):
                        kept[4 * comp + block, index - 1, place, :, lanes] = value
                up, mp, low, m, rp, r = element
                for place, value in enumerate((up, mp, low, m, *rp, *r)):
                    sent[2 * (4 * comp + block) + half, place] = value


def tree(elements, first, last, keep):
    if last - first == 1:
        return elements(first)
    centre = (first + last) // 2
    left, right = tree(elements, first, centre, keep), tree(elements, centre, last, keep)
    whole, a, b, c = joined(left, right)
    keep(centre - 1, a, b, c)
    return whole


def untree(kept, first, last, before, value, give):
    if last - first == 1:
        return
    centre = (first + last) // 2
    a, b, c = kept(centre - 1)
    middle = c + a * before + b * value
    give(centre - 1, middle)
    untree(kept, first, centre, before, middle, give)
    untree(kept, centre, last, middle, value, give)


def chain_forward(received, sent, kept):
    def one(index):
        up, mp, low, m, rp, r = (received[index, place] for place in range(6))
        return up, mp, low, m, [rp], [r]

    def keep(index, a, b, c):
        kept[index, 0], kept[index, 1], kept[index, 2] = a, b, c[0]

    up, mp, low, m, rp, r = tree(one, 0, received.shape[0], keep)
    for place, value in enumerate((up, mp, low, m, *rp, *r)):
        for target in range(sent.shape[0]):
            sent[target, place] = value


def chain_back(received, kept, sent, bound):
    groups, members = received.shape[0], sent.shape[0]
    top = {}

    def one(index):
        up, mp, low, m, rp, r = (received[index, place] for place in range(6))
        return up, mp, low, m, [rp], [r]

    def keep(index, a, b, c):
        top[index] = a, b, c[0]

    def give(index, value):
        bound[index + 1] = value

    up, mp, low, m, rp, r = tree(one, 0, groups, keep)
    zero = jnp.zeros_like(up)
    value = r[0] / (low + m)
    bound[0] = zero
    give(groups - 1, value)
    untree(lambda index: top[index], 0, groups, zero, value, give)
    mine = lax.axis_index("tun") // members
    before, value = bound[mine], bound[mine + 1]

    def end(index, value):
        sent[index, 1] = value
        if index + 1 < members:
            sent[index + 1, 0] = value

    sent[0, 0] = before
    end(members - 1, value)
    untree(lambda index: [kept[index, place] for place in range(3)], 0, members, before, value, end)


def split(value):
    high = value.astype(jnp.bfloat16)
    return high, (value - high.astype(F32)).astype(jnp.bfloat16)


def tunnel_back(received, kept, high, low, out, carried, solved, done):
    for group in range(8):
        comp, block = group // 4, group % 4
        for half in range(2):
            lanes = pl.ds(half * LANES, LANES)
            before, value = received[2 * group + half, 0], received[2 * group + half, 1]
            for index in range(3, -1, -1):
                if index < 3:
                    a, b, c = (kept[group, index, place, :, lanes] for place in range(3))
                    value = c + a * before + b * value
                carried[pl.ds(128 * comp + 32 * index + 8 * block, 8), lanes] = value

    def times(one, two):
        return jnp.dot(one, two[...], preferred_element_type=F32)

    copies = []
    for part in range(4):
        rows = pl.ds(64 * part, 64)
        top, rest = split(carried[rows, :])
        solved[rows, :] = times(top, high) + (times(top, low) + times(rest, high))
        copy = pltpu.make_async_copy(solved.at[rows, :], out.at[rows, :], done.at[part])
        copy.start()
        copies.append(copy)
    for copy in copies:
        copy.wait()


def width_inverse(face, high, low_part):
    count = 256
    step = 1

    def filled(start):
        parts = [face[start + LANES * half : start + LANES * (half + 1)] for half in range(2)]
        return jnp.concatenate([jnp.transpose(jnp.broadcast_to(part.reshape(1, LANES), (LANES, LANES))) for part in parts], axis=0)

    lower, upper = filled(0), filled(1)
    row = lax.broadcasted_iota(jnp.int32, (count, LANES), 0)
    one = jnp.ones((count, LANES), F32)
    m = one + jnp.where(row == 0, lower, 0.0) + jnp.where(row == count - 1, upper, 0.0)
    low, up = jnp.where(row == 0, 0.0, lower), jnp.where(row == count - 1, 0.0, upper)
    column = lax.broadcasted_iota(jnp.int32, (count, LANES), 1)
    rights = [jnp.where(row == column + LANES * half, 1.0, 0.0) for half in range(2)]

    def earlier(value, step):
        return jnp.concatenate([jnp.zeros_like(value[:step]), value[:-step]], axis=0)

    def later(value, step):
        return jnp.concatenate([value[step:], jnp.zeros_like(value[:step])], axis=0)

    while step < count:
        inverse = 1.0 / (low + m + up)
        part = m * inverse
        scaled = [right * inverse for right in rights]
        rights = [
            right + low * earlier(value, step) + up * later(value, step) for right, value in zip(rights, scaled)
        ]
        m, low, up = (
            m + low * earlier(part, step) + up * later(part, step),
            low * earlier(low * inverse, step),
            up * later(up * inverse, step),
        )
        step *= 2
    for half in range(2):
        lanes = pl.ds(half * LANES, LANES)
        top, rest = split(rights[half] / m)
        high[:, lanes] = top
        low_part[:, lanes] = rest


def call(kernel, outs, scratch, *args, place=pltpu.VMEM, out_place=pltpu.VMEM):
    if place is pltpu.HBM:
        args = [pltpu.with_memory_space_constraint(arg, place) for arg in args]
    return pl.pallas_call(
        kernel,
        out_shape=[jax.ShapeDtypeStruct(shape, dtype) for shape, dtype in outs],
        in_specs=[pl.BlockSpec(memory_space=place)] * len(args),
        out_specs=[pl.BlockSpec(memory_space=out_place)] * len(outs),
        scratch_shapes=scratch,
        compiler_params=pltpu.CompilerParams(vmem_limit_bytes=16 * 2**20),
    )(*args)


def room(*shape):
    return pltpu.VMEM(shape, F32)


def per_device(cotangent, tun_cond, tun_flow, heat_loss, hgt_cond, hgt_lift, wid_cond):
    members = 16
    count = lax.axis_size("tun")
    near = [list(range(first, first + members)) for first in range(0, count, members)]
    far = [list(range(first, count, members)) for first in range(members)]
    groups = len(near)

    def exchanged(value, axis, groups=None):
        return lax.all_to_all(value, axis, 0, 0, tiled=True, axis_index_groups=groups)

    def rows(value):
        return value.reshape(-1, 256)

    elements, saved, middle, high, low = call(
        front,
        [((4, 32, 256), F32), ((4, 15, 8, 256), F32), ((16, 256), F32), *[((256, 256), jnp.bfloat16)] * 2],
        [
            room(2, 8, 8, LANES),
            room(2, 256, LANES),
            room(2, 128, LANES),
            room(2, 128, LANES),
            room(257),
            pltpu.SemaphoreType.DMA((7,)),
        ],
        rows(cotangent),
        rows(hgt_cond),
        rows(hgt_lift),
        wid_cond,
        place=pltpu.HBM,
    )
    elements = exchanged(elements, "hgt")
    sent, kept = call(
        height_back,
        [((members, 6, 8, LANES), F32), ((8, 3, 3, 8, 256), F32)],
        [room(5, 8, 256), room(2, 2, 2, 8, LANES), room(2, 256, LANES)],
        elements,
        saved,
        middle,
        rows(tun_cond),
        rows(tun_flow),
        rows(heat_loss),
    )
    received = exchanged(sent, "tun", near)
    sent, chain = call(
        chain_forward, [((groups, 6, 8, LANES), F32), ((members - 1, 3, 8, LANES), F32)], [], received
    )
    received = exchanged(sent, "tun", far)
    [sent] = call(
        chain_back, [((members, 2, 8, LANES), F32)], [room(groups + 1, 8, LANES)], received, chain
    )
    received = exchanged(sent, "tun", near)
    [solved] = call(
        tunnel_back,
        [((256, 256), F32)],
        [room(256, 256), room(256, 256), pltpu.SemaphoreType.DMA((4,))],
        received,
        kept,
        high,
        low,
        out_place=pltpu.HBM,
    )
    return solved.reshape(cotangent.shape)


def solution(mesh):
    in_specs = (
        P(None, "tun", "hgt", None),
        P("tun", "hgt", None),
        P("tun", "hgt", None),
        P("tun", "hgt", None),
        P("tun", "hgt", None),
        P("tun", "hgt", None),
        P(),
    )
    out_specs = P(None, "tun", "hgt", None)
    return jax.shard_map(
        per_device, mesh=mesh, in_specs=in_specs, out_specs=out_specs, check_vma=False
    )
```

```python
import jax
import jax.numpy as jnp
from jax import lax
from jax.experimental import pallas as pl
from jax.experimental.pallas import tpu as pltpu
from jax.sharding import PartitionSpec as P

F32 = jnp.float32
LANES = 128

HEIGHT_ORDER = (2, 3, 0, 1)
JOIN_ORDER = (4, 5, 6, 7, 8, 9, 10, 11, 12, 13, 14, 15, 0, 1, 2, 3)
FAR_ORDER = (5, 6, 7, 0, 1, 2, 3, 4)
BACK_ORDER = (4, 5, 6, 7, 8, 9, 10, 11, 12, 13, 14, 15, 0, 1, 2, 3)


def places(order):
    return [order.index(member) for member in range(len(order))]


def joined(element, following):
    up, mp, low, m, rp, r = element
    next_up, next_mp, next_low, next_m, next_rp, next_r = following
    mid = m + next_mp
    inverse = 1.0 / (mid + low + next_up)
    a, b, mid = low * inverse, next_up * inverse, mid * inverse
    c = [(one + two) * inverse for one, two in zip(r, next_rp)]
    whole = (
        up * b,
        mp + up * mid,
        next_low * a,
        next_m + next_low * mid,
        [one + up * two for one, two in zip(rp, c)],
        [one + next_low * two for one, two in zip(next_r, c)],
    )
    return whole, a, b, c


def front(field, cond, lift, wide, elements, saved, middle, high, rest, pieces, fields, conds, lifts, face, done):
    face_copy = pltpu.make_async_copy(wide, face, done.at[6])
    face_copy.start()
    copies = []
    for source, target in ((field, fields), (cond, conds), (lift, lifts)):
        for half in range(2):
            copy = pltpu.make_async_copy(
                source.at[:, pl.ds(half * LANES, LANES)], target.at[half], done.at[len(copies)]
            )
            copy.start()
            copies.append(copy)
    face_copy.wait()
    width_inverse(face, high, rest)
    for copy in copies:
        copy.wait()
    height_forward(elements, saved, middle, pieces, fields, conds, lifts)


def height_forward(elements, saved, middle, pieces, fields, conds, lifts):
    lower = [pl.ds(0, 4, stride=2), pl.ds(1, 4, stride=2)]
    for half in range(2):
        lanes = pl.ds(half * LANES, LANES)


        def cell(ref, index, base=0):
            return ref[half, pl.ds(base + index, 8, stride=16), :]

        def one(index):
            k = cell(conds, index)
            return (
                k + cell(lifts, index),
                jnp.zeros_like(k),
                k,
                jnp.ones_like(k),
                [jnp.zeros_like(k)] * 2,
                [cell(fields, index), cell(fields, index, 128)],
            )

        element = one(0)
        for index in range(1, 16):
            element, a, b, c = joined(element, one(index))
            for place, part in enumerate((a, b, *c)):
                saved[place, index - 1, :, lanes] = part
        up, mp, low, m, rp, r = element
        for place, part in enumerate((up, mp, low, m, *rp, *r)):
            pieces[half, place] = part

        def sub(which):
            up, mp, low, m, rp0, rp1, r0, r1 = (pieces[half, place, lower[which]] for place in range(8))
            return up, mp, low, m, [rp0, rp1], [r0, r1]

        whole, a, b, c = joined(sub(0), sub(1))
        for place, part in enumerate((a, b, *c)):
            middle[pl.ds(4 * place, 4), lanes] = part
        up, mp, low, m, rp, r = whole
        for place, part in enumerate((up, mp, low, m, *rp, *r)):
            for target in range(4):
                elements[target, pl.ds(4 * place, 4), lanes] = part


def height_back(elements, saved, middle, cond, flow, loss, sent, kept, bound, ends, lifted):
    def part(source, place, rows=4):
        return elements[heights[source], pl.ds(4 * place, rows), :]

    rows_of, heights, targets = [], places(HEIGHT_ORDER), places(JOIN_ORDER)
    for source in range(4):
        low, m, r = part(source, 2), part(source, 3), part(source, 6, 8)
        if source == 0:
            low, m = jnp.zeros_like(low), m + low
        up = jnp.zeros_like(low)
        if source < 3:
            up, m, r = part(source + 1, 0), m + part(source + 1, 1), r + part(source + 1, 4, 8)
        rows_of.append([low, m, up, r])

    def twice(value):
        return jnp.concatenate([value, value], axis=0)

    scale = []
    for source in range(4):
        low, m, up, r = rows_of[source]
        inverse = 1.0 / (m + up)
        scale.append((twice(up * inverse), r * twice(inverse)))
        if source < 3:
            after = rows_of[source + 1]
            after[1] = after[1] + after[0] * (m * inverse)
            after[3] = after[3] + twice(after[0]) * scale[source][1]
    bound[0] = jnp.zeros_like(bound[0])
    value = scale[3][1]
    bound[4] = value
    for source in (2, 1, 0):
        value = scale[source][1] + scale[source][0] * value
        bound[source + 1] = value
    mine = lax.axis_index("hgt")
    before, last = bound[mine], bound[mine + 1]
    a, b, c = middle[0:4, :], middle[4:8, :], middle[8:16, :]
    centre = c + twice(a) * before + twice(b) * last
    even, odd = pl.ds(0, 4, stride=2), pl.ds(1, 4, stride=2)
    for half in range(2):
        lanes = pl.ds(half * LANES, LANES)
        cut = slice(half * LANES, (half + 1) * LANES)
        for comp in range(2):
            rows = slice(4 * comp, 4 * comp + 4)
            ends[half, comp, 0, even] = before[rows, cut]
            ends[half, comp, 0, odd] = centre[rows, cut]
            ends[half, comp, 1, even] = centre[rows, cut]
            ends[half, comp, 1, odd] = last[rows, cut]
            start, value = ends[half, comp, 0], ends[half, comp, 1]
            lifted[half, pl.ds(128 * comp + 15, 8, stride=16), :] = value
            for index in range(14, -1, -1):
                value = (
                    saved[2 + comp, index, :, lanes]
                    + saved[0, index, :, lanes] * start
                    + saved[1, index, :, lanes] * value
                )
                lifted[half, pl.ds(128 * comp + index, 8, stride=16), :] = value
    for block in range(4):
        for half in range(2):
            lanes = pl.ds(half * LANES, LANES)
            for comp in range(2):

                def one(index):
                    rows = pl.ds(32 * index + 8 * block, 8)
                    k = cond[rows, lanes]
                    m = 1.0 + loss[rows, lanes] if comp == 0 else jnp.ones_like(k)
                    r = lifted[half, pl.ds(128 * comp + 32 * index + 8 * block, 8), :]
                    zero = jnp.zeros_like(k)
                    return k + flow[rows, lanes], zero, k, m, [zero], [r]

                element = one(0)
                for index in range(1, 4):
                    element, a, b, c = joined(element, one(index))
                    for place, value in enumerate((a, b, *c)):
                        kept[4 * comp + block, index - 1, place, :, lanes] = value
                up, mp, low, m, rp, r = element
                for place, value in enumerate((up, mp, low, m, *rp, *r)):
                    sent[targets[2 * (4 * comp + block) + half], place] = value


def tree(elements, first, last, keep):
    if last - first == 1:
        return elements(first)
    centre = (first + last) // 2
    left, right = tree(elements, first, centre, keep), tree(elements, centre, last, keep)
    whole, a, b, c = joined(left, right)
    keep(centre - 1, a, b, c)
    return whole


def untree(kept, first, last, before, value, give):
    if last - first == 1:
        return
    centre = (first + last) // 2
    a, b, c = kept(centre - 1)
    middle = c + a * before + b * value
    give(centre - 1, middle)
    untree(kept, first, centre, before, middle, give)
    untree(kept, centre, last, middle, value, give)


def chain_forward(received, sent, kept):
    sources = places(JOIN_ORDER)

    def one(index):
        up, mp, low, m, rp, r = (received[sources[index], place] for place in range(6))
        return up, mp, low, m, [rp], [r]

    def keep(index, a, b, c):
        kept[index, 0], kept[index, 1], kept[index, 2] = a, b, c[0]

    up, mp, low, m, rp, r = tree(one, 0, received.shape[0], keep)
    for place, value in enumerate((up, mp, low, m, *rp, *r)):
        for target in range(sent.shape[0]):
            sent[target, place] = value


def chain_back(received, kept, sent, bound):
    groups, members = received.shape[0], sent.shape[0]
    sources, targets = places(FAR_ORDER), places(BACK_ORDER)
    top = {}

    def one(index):
        up, mp, low, m, rp, r = (received[sources[index], place] for place in range(6))
        return up, mp, low, m, [rp], [r]

    def keep(index, a, b, c):
        top[index] = a, b, c[0]

    def give(index, value):
        bound[index + 1] = value

    up, mp, low, m, rp, r = tree(one, 0, groups, keep)
    zero = jnp.zeros_like(up)
    value = r[0] / (low + m)
    bound[0] = zero
    give(groups - 1, value)
    untree(lambda index: top[index], 0, groups, zero, value, give)
    mine = lax.axis_index("tun") // members
    before, value = bound[mine], bound[mine + 1]

    def end(index, value):
        sent[targets[index], 1] = value
        if index + 1 < members:
            sent[targets[index + 1], 0] = value

    sent[targets[0], 0] = before
    end(members - 1, value)
    untree(lambda index: [kept[index, place] for place in range(3)], 0, members, before, value, end)


def split(value):
    high = value.astype(jnp.bfloat16)
    return high, (value - high.astype(F32)).astype(jnp.bfloat16)


def tunnel_back(received, kept, high, low, out, carried, solved, done):
    sources = places(BACK_ORDER)
    for group in range(8):
        comp, block = group // 4, group % 4
        for half in range(2):
            lanes = pl.ds(half * LANES, LANES)
            source = sources[2 * group + half]
            before, value = received[source, 0], received[source, 1]
            for index in range(3, -1, -1):
                if index < 3:
                    a, b, c = (kept[group, index, place, :, lanes] for place in range(3))
                    value = c + a * before + b * value
                carried[pl.ds(128 * comp + 32 * index + 8 * block, 8), lanes] = value

    def times(one, two):
        return jnp.dot(one, two[...], preferred_element_type=F32)

    copies = []
    for part in range(4):
        rows = pl.ds(64 * part, 64)
        top, rest = split(carried[rows, :])
        solved[rows, :] = times(top, high) + (times(top, low) + times(rest, high))
        copy = pltpu.make_async_copy(solved.at[rows, :], out.at[rows, :], done.at[part])
        copy.start()
        copies.append(copy)
    for copy in copies:
        copy.wait()


def width_inverse(face, high, low_part):
    count = 256
    step = 1

    def filled(start):
        parts = [face[start + LANES * half : start + LANES * (half + 1)] for half in range(2)]
        return jnp.concatenate([jnp.transpose(jnp.broadcast_to(part.reshape(1, LANES), (LANES, LANES))) for part in parts], axis=0)

    lower, upper = filled(0), filled(1)
    row = lax.broadcasted_iota(jnp.int32, (count, LANES), 0)
    one = jnp.ones((count, LANES), F32)
    m = one + jnp.where(row == 0, lower, 0.0) + jnp.where(row == count - 1, upper, 0.0)
    low, up = jnp.where(row == 0, 0.0, lower), jnp.where(row == count - 1, 0.0, upper)
    column = lax.broadcasted_iota(jnp.int32, (count, LANES), 1)
    rights = [jnp.where(row == column + LANES * half, 1.0, 0.0) for half in range(2)]

    def earlier(value, step):
        return jnp.concatenate([jnp.zeros_like(value[:step]), value[:-step]], axis=0)

    def later(value, step):
        return jnp.concatenate([value[step:], jnp.zeros_like(value[:step])], axis=0)

    while step < count:
        inverse = 1.0 / (low + m + up)
        part = m * inverse
        scaled = [right * inverse for right in rights]
        rights = [
            right + low * earlier(value, step) + up * later(value, step) for right, value in zip(rights, scaled)
        ]
        m, low, up = (
            m + low * earlier(part, step) + up * later(part, step),
            low * earlier(low * inverse, step),
            up * later(up * inverse, step),
        )
        step *= 2
    for half in range(2):
        lanes = pl.ds(half * LANES, LANES)
        top, rest = split(rights[half] / m)
        high[:, lanes] = top
        low_part[:, lanes] = rest


def call(kernel, outs, scratch, *args, place=pltpu.VMEM, out_place=pltpu.VMEM):
    if place is pltpu.HBM:
        args = [pltpu.with_memory_space_constraint(arg, place) for arg in args]
    return pl.pallas_call(
        kernel,
        out_shape=[jax.ShapeDtypeStruct(shape, dtype) for shape, dtype in outs],
        in_specs=[pl.BlockSpec(memory_space=place)] * len(args),
        out_specs=[pl.BlockSpec(memory_space=out_place)] * len(outs),
        scratch_shapes=scratch,
        compiler_params=pltpu.CompilerParams(vmem_limit_bytes=16 * 2**20),
    )(*args)


def room(*shape):
    return pltpu.VMEM(shape, F32)


def per_device(cotangent, tun_cond, tun_flow, heat_loss, hgt_cond, hgt_lift, wid_cond):
    members = len(JOIN_ORDER)
    count = lax.axis_size("tun")
    join = [[first + member for member in JOIN_ORDER] for first in range(0, count, members)]
    back = [[first + member for member in BACK_ORDER] for first in range(0, count, members)]
    far = [[first + members * group for group in FAR_ORDER] for first in range(members)]
    groups = len(FAR_ORDER)

    def exchanged(value, axis, groups=None):
        return lax.all_to_all(value, axis, 0, 0, tiled=True, axis_index_groups=groups)

    def rows(value):
        return value.reshape(-1, 256)

    elements, saved, middle, high, low = call(
        front,
        [((4, 32, 256), F32), ((4, 15, 8, 256), F32), ((16, 256), F32), *[((256, 256), jnp.bfloat16)] * 2],
        [
            room(2, 8, 8, LANES),
            room(2, 256, LANES),
            room(2, 128, LANES),
            room(2, 128, LANES),
            room(257),
            pltpu.SemaphoreType.DMA((7,)),
        ],
        rows(cotangent),
        rows(hgt_cond),
        rows(hgt_lift),
        wid_cond,
        place=pltpu.HBM,
    )
    elements = exchanged(elements, "hgt", [list(HEIGHT_ORDER)])
    sent, kept = call(
        height_back,
        [((members, 6, 8, LANES), F32), ((8, 3, 3, 8, 256), F32)],
        [room(5, 8, 256), room(2, 2, 2, 8, LANES), room(2, 256, LANES)],
        elements,
        saved,
        middle,
        rows(tun_cond),
        rows(tun_flow),
        rows(heat_loss),
    )
    received = exchanged(sent, "tun", join)
    sent, chain = call(
        chain_forward, [((groups, 6, 8, LANES), F32), ((members - 1, 3, 8, LANES), F32)], [], received
    )
    received = exchanged(sent, "tun", far)
    [sent] = call(
        chain_back, [((members, 2, 8, LANES), F32)], [room(groups + 1, 8, LANES)], received, chain
    )
    received = exchanged(sent, "tun", back)
    [solved] = call(
        tunnel_back,
        [((256, 256), F32)],
        [room(256, 256), room(256, 256), pltpu.SemaphoreType.DMA((4,))],
        received,
        kept,
        high,
        low,
        out_place=pltpu.HBM,
    )
    return solved.reshape(cotangent.shape)


def solution(mesh):
    in_specs = (
        P(None, "tun", "hgt", None),
        P("tun", "hgt", None),
        P("tun", "hgt", None),
        P("tun", "hgt", None),
        P("tun", "hgt", None),
        P("tun", "hgt", None),
        P(),
    )
    out_specs = P(None, "tun", "hgt", None)
    return jax.shard_map(
        per_device, mesh=mesh, in_specs=in_specs, out_specs=out_specs, check_vma=False
    )
```

```python
import jax
import jax.numpy as jnp
from jax import lax
from jax.experimental import pallas as pl
from jax.experimental.pallas import tpu as pltpu
from jax.sharding import PartitionSpec as P

F32 = jnp.float32
LANES = 128
EARLY_LAYERS = 6

HEIGHT_ORDER = (2, 3, 0, 1)
JOIN_ORDER = (13, 14, 15, 0, 1, 2, 3, 4, 5, 6, 7, 8, 9, 10, 11, 12)
FAR_ORDER = (5, 6, 7, 0, 1, 2, 3, 4)
BACK_ORDER = (5, 6, 7, 8, 9, 10, 11, 12, 13, 14, 15, 0, 1, 2, 3, 4)


def places(order):
    return [order.index(member) for member in range(len(order))]


def joined(element, following):
    up, mp, low, m, rp, r = element
    next_up, next_mp, next_low, next_m, next_rp, next_r = following
    mid = m + next_mp
    inverse = 1.0 / (mid + low + next_up)
    a, b, mid = low * inverse, next_up * inverse, mid * inverse
    c = [(one + two) * inverse for one, two in zip(r, next_rp)]
    whole = (
        up * b,
        mp + up * mid,
        next_low * a,
        next_m + next_low * mid,
        [one + up * two for one, two in zip(rp, c)],
        [one + next_low * two for one, two in zip(next_r, c)],
    )
    return whole, a, b, c


def early():
    return lax.axis_index("tun") // 8 < EARLY_LAYERS


def front(field, cond, lift, wide, elements, saved, middle, high, rest, face, pieces, fields, conds, lifts, done):
    face_copy = pltpu.make_async_copy(wide, face, done.at[6])
    face_copy.start()
    copies = []
    for source, target in ((field, fields), (cond, conds), (lift, lifts)):
        for half in range(2):
            copy = pltpu.make_async_copy(
                source.at[:, pl.ds(half * LANES, LANES)], target.at[half], done.at[len(copies)]
            )
            copy.start()
            copies.append(copy)
    face_copy.wait()

    @pl.when(early())
    def _():
        width_inverse(face, high, rest)

    for copy in copies:
        copy.wait()
    height_forward(elements, saved, middle, pieces, fields, conds, lifts)


def height_forward(elements, saved, middle, pieces, fields, conds, lifts):
    lower = [pl.ds(0, 4, stride=2), pl.ds(1, 4, stride=2)]
    for half in range(2):
        lanes = pl.ds(half * LANES, LANES)


        def cell(ref, index, base=0):
            return ref[half, pl.ds(base + index, 8, stride=16), :]

        def one(index):
            k = cell(conds, index)
            return (
                k + cell(lifts, index),
                jnp.zeros_like(k),
                k,
                jnp.ones_like(k),
                [jnp.zeros_like(k)] * 2,
                [cell(fields, index), cell(fields, index, 128)],
            )

        element = one(0)
        for index in range(1, 16):
            element, a, b, c = joined(element, one(index))
            for place, part in enumerate((a, b, *c)):
                saved[place, index - 1, :, lanes] = part
        up, mp, low, m, rp, r = element
        for place, part in enumerate((up, mp, low, m, *rp, *r)):
            pieces[half, place] = part

        def sub(which):
            up, mp, low, m, rp0, rp1, r0, r1 = (pieces[half, place, lower[which]] for place in range(8))
            return up, mp, low, m, [rp0, rp1], [r0, r1]

        whole, a, b, c = joined(sub(0), sub(1))
        for place, part in enumerate((a, b, *c)):
            middle[pl.ds(4 * place, 4), lanes] = part
        up, mp, low, m, rp, r = whole
        for place, part in enumerate((up, mp, low, m, *rp, *r)):
            for target in range(4):
                elements[target, pl.ds(4 * place, 4), lanes] = part


def height_back(elements, saved, middle, cond, flow, loss, sent, kept, bound, ends, lifted):
    def part(source, place, rows=4):
        return elements[heights[source], pl.ds(4 * place, rows), :]

    rows_of, heights, targets = [], places(HEIGHT_ORDER), places(JOIN_ORDER)
    for source in range(4):
        low, m, r = part(source, 2), part(source, 3), part(source, 6, 8)
        if source == 0:
            low, m = jnp.zeros_like(low), m + low
        up = jnp.zeros_like(low)
        if source < 3:
            up, m, r = part(source + 1, 0), m + part(source + 1, 1), r + part(source + 1, 4, 8)
        rows_of.append([low, m, up, r])

    def twice(value):
        return jnp.concatenate([value, value], axis=0)

    scale = []
    for source in range(4):
        low, m, up, r = rows_of[source]
        inverse = 1.0 / (m + up)
        scale.append((twice(up * inverse), r * twice(inverse)))
        if source < 3:
            after = rows_of[source + 1]
            after[1] = after[1] + after[0] * (m * inverse)
            after[3] = after[3] + twice(after[0]) * scale[source][1]
    bound[0] = jnp.zeros_like(bound[0])
    value = scale[3][1]
    bound[4] = value
    for source in (2, 1, 0):
        value = scale[source][1] + scale[source][0] * value
        bound[source + 1] = value
    mine = lax.axis_index("hgt")
    before, last = bound[mine], bound[mine + 1]
    a, b, c = middle[0:4, :], middle[4:8, :], middle[8:16, :]
    centre = c + twice(a) * before + twice(b) * last
    even, odd = pl.ds(0, 4, stride=2), pl.ds(1, 4, stride=2)
    for half in range(2):
        lanes = pl.ds(half * LANES, LANES)
        cut = slice(half * LANES, (half + 1) * LANES)
        for comp in range(2):
            rows = slice(4 * comp, 4 * comp + 4)
            ends[half, comp, 0, even] = before[rows, cut]
            ends[half, comp, 0, odd] = centre[rows, cut]
            ends[half, comp, 1, even] = centre[rows, cut]
            ends[half, comp, 1, odd] = last[rows, cut]
            start, value = ends[half, comp, 0], ends[half, comp, 1]
            lifted[half, pl.ds(128 * comp + 15, 8, stride=16), :] = value
            for index in range(14, -1, -1):
                value = (
                    saved[2 + comp, index, :, lanes]
                    + saved[0, index, :, lanes] * start
                    + saved[1, index, :, lanes] * value
                )
                lifted[half, pl.ds(128 * comp + index, 8, stride=16), :] = value
    for block in range(4):
        for half in range(2):
            lanes = pl.ds(half * LANES, LANES)
            for comp in range(2):

                def one(index):
                    rows = pl.ds(32 * index + 8 * block, 8)
                    k = cond[rows, lanes]
                    m = 1.0 + loss[rows, lanes] if comp == 0 else jnp.ones_like(k)
                    r = lifted[half, pl.ds(128 * comp + 32 * index + 8 * block, 8), :]
                    zero = jnp.zeros_like(k)
                    return k + flow[rows, lanes], zero, k, m, [zero], [r]

                element = one(0)
                for index in range(1, 4):
                    element, a, b, c = joined(element, one(index))
                    for place, value in enumerate((a, b, *c)):
                        kept[4 * comp + block, index - 1, place, :, lanes] = value
                up, mp, low, m, rp, r = element
                for place, value in enumerate((up, mp, low, m, *rp, *r)):
                    sent[targets[2 * (4 * comp + block) + half], place] = value


def tree(elements, first, last, keep):
    if last - first == 1:
        return elements(first)
    centre = (first + last) // 2
    left, right = tree(elements, first, centre, keep), tree(elements, centre, last, keep)
    whole, a, b, c = joined(left, right)
    keep(centre - 1, a, b, c)
    return whole


def untree(kept, first, last, before, value, give):
    if last - first == 1:
        return
    centre = (first + last) // 2
    a, b, c = kept(centre - 1)
    middle = c + a * before + b * value
    give(centre - 1, middle)
    untree(kept, first, centre, before, middle, give)
    untree(kept, centre, last, middle, value, give)


def chain_forward(received, sent, kept):
    sources = places(JOIN_ORDER)

    def one(index):
        up, mp, low, m, rp, r = (received[sources[index], place] for place in range(6))
        return up, mp, low, m, [rp], [r]

    def keep(index, a, b, c):
        kept[index, 0], kept[index, 1], kept[index, 2] = a, b, c[0]

    up, mp, low, m, rp, r = tree(one, 0, received.shape[0], keep)
    for place, value in enumerate((up, mp, low, m, *rp, *r)):
        for target in range(sent.shape[0]):
            sent[target, place] = value


def chain_back(received, kept, sent, bound):
    groups, members = received.shape[0], sent.shape[0]
    sources, targets = places(FAR_ORDER), places(BACK_ORDER)
    top = {}

    def one(index):
        up, mp, low, m, rp, r = (received[sources[index], place] for place in range(6))
        return up, mp, low, m, [rp], [r]

    def keep(index, a, b, c):
        top[index] = a, b, c[0]

    def give(index, value):
        bound[index + 1] = value

    up, mp, low, m, rp, r = tree(one, 0, groups, keep)
    zero = jnp.zeros_like(up)
    value = r[0] / (low + m)
    bound[0] = zero
    give(groups - 1, value)
    untree(lambda index: top[index], 0, groups, zero, value, give)
    mine = lax.axis_index("tun") // members
    before, value = bound[mine], bound[mine + 1]

    def end(index, value):
        sent[targets[index], 1] = value
        if index + 1 < members:
            sent[targets[index + 1], 0] = value

    sent[targets[0], 0] = before
    end(members - 1, value)
    untree(lambda index: [kept[index, place] for place in range(3)], 0, members, before, value, end)


def split(value):
    high = value.astype(jnp.bfloat16)
    return high, (value - high.astype(F32)).astype(jnp.bfloat16)


def tunnel_back(received, kept, high, low, face, out, carried, solved, top_matrix, rest_matrix, done):
    @pl.when(early())
    def _():
        top_matrix[...], rest_matrix[...] = high[...], low[...]

    @pl.when(jnp.logical_not(early()))
    def _():
        width_inverse(face, top_matrix, rest_matrix)

    sources = places(BACK_ORDER)
    for group in range(8):
        comp, block = group // 4, group % 4
        for half in range(2):
            lanes = pl.ds(half * LANES, LANES)
            source = sources[2 * group + half]
            before, value = received[source, 0], received[source, 1]
            for index in range(3, -1, -1):
                if index < 3:
                    a, b, c = (kept[group, index, place, :, lanes] for place in range(3))
                    value = c + a * before + b * value
                carried[pl.ds(128 * comp + 32 * index + 8 * block, 8), lanes] = value

    def times(one, two):
        return jnp.dot(one, two[...], preferred_element_type=F32)

    top, rest = split(carried[...])
    both = times(jnp.concatenate([top, rest], axis=0), top_matrix)
    solved[...] = both[:256] + (times(top, rest_matrix) + both[256:])
    copies = []
    for part in range(4):
        rows = pl.ds(64 * part, 64)
        copy = pltpu.make_async_copy(solved.at[rows, :], out.at[rows, :], done.at[part])
        copy.start()
        copies.append(copy)
    for copy in copies:
        copy.wait()


def width_inverse(face, high, low_part):
    count = 256
    step = 1

    def filled(start):
        parts = [face[start + LANES * half : start + LANES * (half + 1)] for half in range(2)]
        return jnp.concatenate([jnp.transpose(jnp.broadcast_to(part.reshape(1, LANES), (LANES, LANES))) for part in parts], axis=0)

    lower, upper = filled(0), filled(1)
    row = lax.broadcasted_iota(jnp.int32, (count, LANES), 0)
    one = jnp.ones((count, LANES), F32)
    m = one + jnp.where(row == 0, lower, 0.0) + jnp.where(row == count - 1, upper, 0.0)
    low, up = jnp.where(row == 0, 0.0, lower), jnp.where(row == count - 1, 0.0, upper)
    column = lax.broadcasted_iota(jnp.int32, (count, LANES), 1)
    rights = [jnp.where(row == column + LANES * half, 1.0, 0.0) for half in range(2)]

    def earlier(value, step):
        return jnp.concatenate([jnp.zeros_like(value[:step]), value[:-step]], axis=0)

    def later(value, step):
        return jnp.concatenate([value[step:], jnp.zeros_like(value[:step])], axis=0)

    while step < count:
        inverse = 1.0 / (low + m + up)
        part = m * inverse
        scaled = [right * inverse for right in rights]
        rights = [
            right + low * earlier(value, step) + up * later(value, step) for right, value in zip(rights, scaled)
        ]
        m, low, up = (
            m + low * earlier(part, step) + up * later(part, step),
            low * earlier(low * inverse, step),
            up * later(up * inverse, step),
        )
        step *= 2
    for half in range(2):
        lanes = pl.ds(half * LANES, LANES)
        top, rest = split(rights[half] / m)
        high[:, lanes] = top
        low_part[:, lanes] = rest


def call(kernel, outs, scratch, *args, place=pltpu.VMEM, out_place=pltpu.VMEM):
    if place is pltpu.HBM:
        args = [pltpu.with_memory_space_constraint(arg, place) for arg in args]
    return pl.pallas_call(
        kernel,
        out_shape=[jax.ShapeDtypeStruct(shape, dtype) for shape, dtype in outs],
        in_specs=[pl.BlockSpec(memory_space=place)] * len(args),
        out_specs=[pl.BlockSpec(memory_space=out_place)] * len(outs),
        scratch_shapes=scratch,
        compiler_params=pltpu.CompilerParams(vmem_limit_bytes=16 * 2**20),
    )(*args)


def room(*shape):
    return pltpu.VMEM(shape, F32)


def per_device(cotangent, tun_cond, tun_flow, heat_loss, hgt_cond, hgt_lift, wid_cond):
    members = len(JOIN_ORDER)
    count = lax.axis_size("tun")
    join = [[first + member for member in JOIN_ORDER] for first in range(0, count, members)]
    back = [[first + member for member in BACK_ORDER] for first in range(0, count, members)]
    far = [[first + members * group for group in FAR_ORDER] for first in range(members)]
    groups = len(FAR_ORDER)

    def exchanged(value, axis, groups=None):
        return lax.all_to_all(value, axis, 0, 0, tiled=True, axis_index_groups=groups)

    def rows(value):
        return value.reshape(-1, 256)

    elements, saved, middle, high, low, face = call(
        front,
        [((4, 32, 256), F32), ((4, 15, 8, 256), F32), ((16, 256), F32), *[((256, 256), jnp.bfloat16)] * 2, ((257,), F32)],
        [
            room(2, 8, 8, LANES),
            room(2, 256, LANES),
            room(2, 128, LANES),
            room(2, 128, LANES),
            pltpu.SemaphoreType.DMA((7,)),
        ],
        rows(cotangent),
        rows(hgt_cond),
        rows(hgt_lift),
        wid_cond,
        place=pltpu.HBM,
    )
    elements = exchanged(elements, "hgt", [list(HEIGHT_ORDER)])
    sent, kept = call(
        height_back,
        [((members, 6, 8, LANES), F32), ((8, 3, 3, 8, 256), F32)],
        [room(5, 8, 256), room(2, 2, 2, 8, LANES), room(2, 256, LANES)],
        elements,
        saved,
        middle,
        rows(tun_cond),
        rows(tun_flow),
        rows(heat_loss),
    )
    received = exchanged(sent, "tun", join)
    sent, chain = call(
        chain_forward, [((groups, 6, 8, LANES), F32), ((members - 1, 3, 8, LANES), F32)], [], received
    )
    received = exchanged(sent, "tun", far)
    [sent] = call(
        chain_back, [((members, 2, 8, LANES), F32)], [room(groups + 1, 8, LANES)], received, chain
    )
    received = exchanged(sent, "tun", back)
    [solved] = call(
        tunnel_back,
        [((256, 256), F32)],
        [
            room(256, 256),
            room(256, 256),
            pltpu.VMEM((256, 256), jnp.bfloat16),
            pltpu.VMEM((256, 256), jnp.bfloat16),
            pltpu.SemaphoreType.DMA((4,)),
        ],
        received,
        kept,
        high,
        low,
        face,
        out_place=pltpu.HBM,
    )
    return solved.reshape(cotangent.shape)


def solution(mesh):
    in_specs = (
        P(None, "tun", "hgt", None),
        P("tun", "hgt", None),
        P("tun", "hgt", None),
        P("tun", "hgt", None),
        P("tun", "hgt", None),
        P("tun", "hgt", None),
        P(),
    )
    out_specs = P(None, "tun", "hgt", None)
    return jax.shard_map(
        per_device, mesh=mesh, in_specs=in_specs, out_specs=out_specs, check_vma=False
    )
```

```python
import jax
import jax.numpy as jnp
from jax import lax
from jax.experimental import pallas as pl
from jax.experimental.pallas import tpu as pltpu
from jax.sharding import PartitionSpec as P

F32 = jnp.float32
LANES = 128
EARLY_LAYERS = 6

HEIGHT_ORDER = (2, 3, 0, 1)
JOIN_ORDER = (10, 11, 12, 13, 14, 15, 0, 1, 2, 3, 4, 5, 6, 7, 8, 9)
FAR_ORDER = (2, 3, 0, 1)
BACK_ORDER = (21, 22, 23, 24, 25, 26, 27, 28, 29, 30, 31, 0, 1, 2, 3, 4, 5, 6, 7, 8, 9, 10, 11, 12, 13, 14, 15, 16, 17, 18, 19, 20)


def places(order):
    return [order.index(member) for member in range(len(order))]


def joined(element, following):
    up, mp, low, m, rp, r = element
    next_up, next_mp, next_low, next_m, next_rp, next_r = following
    mid = m + next_mp
    inverse = 1.0 / (mid + low + next_up)
    a, b, mid = low * inverse, next_up * inverse, mid * inverse
    c = [(one + two) * inverse for one, two in zip(r, next_rp)]
    whole = (
        up * b,
        mp + up * mid,
        next_low * a,
        next_m + next_low * mid,
        [one + up * two for one, two in zip(rp, c)],
        [one + next_low * two for one, two in zip(next_r, c)],
    )
    return whole, a, b, c


def early():
    return lax.axis_index("tun") // 8 < EARLY_LAYERS


def front(field, cond, lift, wide, elements, saved, middle, high, rest, face, pieces, fields, conds, lifts, done):
    face_copy = pltpu.make_async_copy(wide, face, done.at[6])
    face_copy.start()
    copies = []
    for source, target in ((field, fields), (cond, conds), (lift, lifts)):
        for half in range(2):
            copy = pltpu.make_async_copy(
                source.at[:, pl.ds(half * LANES, LANES)], target.at[half], done.at[len(copies)]
            )
            copy.start()
            copies.append(copy)
    face_copy.wait()

    @pl.when(early())
    def _():
        width_inverse(face, high, rest)

    for copy in copies:
        copy.wait()
    height_forward(elements, saved, middle, pieces, fields, conds, lifts)


def height_forward(elements, saved, middle, pieces, fields, conds, lifts):
    lower = [pl.ds(0, 4, stride=2), pl.ds(1, 4, stride=2)]
    for half in range(2):
        lanes = pl.ds(half * LANES, LANES)


        def cell(ref, index, base=0):
            return ref[half, pl.ds(base + index, 8, stride=16), :]

        def one(index):
            k = cell(conds, index)
            return (
                k + cell(lifts, index),
                jnp.zeros_like(k),
                k,
                jnp.ones_like(k),
                [jnp.zeros_like(k)] * 2,
                [cell(fields, index), cell(fields, index, 128)],
            )

        element = one(0)
        for index in range(1, 16):
            element, a, b, c = joined(element, one(index))
            for place, part in enumerate((a, b, *c)):
                saved[place, index - 1, :, lanes] = part
        up, mp, low, m, rp, r = element
        for place, part in enumerate((up, mp, low, m, *rp, *r)):
            pieces[half, place] = part

        def sub(which):
            up, mp, low, m, rp0, rp1, r0, r1 = (pieces[half, place, lower[which]] for place in range(8))
            return up, mp, low, m, [rp0, rp1], [r0, r1]

        whole, a, b, c = joined(sub(0), sub(1))
        for place, part in enumerate((a, b, *c)):
            middle[pl.ds(4 * place, 4), lanes] = part
        up, mp, low, m, rp, r = whole
        for place, part in enumerate((up, mp, low, m, *rp, *r)):
            for target in range(4):
                elements[target, pl.ds(4 * place, 4), lanes] = part


def height_back(elements, saved, middle, cond, flow, loss, sent, kept, bound, ends, lifted):
    def part(source, place, rows=4):
        return elements[heights[source], pl.ds(4 * place, rows), :]

    rows_of, heights = [], places(HEIGHT_ORDER)
    for source in range(4):
        low, m, r = part(source, 2), part(source, 3), part(source, 6, 8)
        if source == 0:
            low, m = jnp.zeros_like(low), m + low
        up = jnp.zeros_like(low)
        if source < 3:
            up, m, r = part(source + 1, 0), m + part(source + 1, 1), r + part(source + 1, 4, 8)
        rows_of.append([low, m, up, r])

    def twice(value):
        return jnp.concatenate([value, value], axis=0)

    scale = []
    for source in range(4):
        low, m, up, r = rows_of[source]
        inverse = 1.0 / (m + up)
        scale.append((twice(up * inverse), r * twice(inverse)))
        if source < 3:
            after = rows_of[source + 1]
            after[1] = after[1] + after[0] * (m * inverse)
            after[3] = after[3] + twice(after[0]) * scale[source][1]
    bound[0] = jnp.zeros_like(bound[0])
    value = scale[3][1]
    bound[4] = value
    for source in (2, 1, 0):
        value = scale[source][1] + scale[source][0] * value
        bound[source + 1] = value
    mine = lax.axis_index("hgt")
    before, last = bound[mine], bound[mine + 1]
    a, b, c = middle[0:4, :], middle[4:8, :], middle[8:16, :]
    centre = c + twice(a) * before + twice(b) * last
    even, odd = pl.ds(0, 4, stride=2), pl.ds(1, 4, stride=2)
    for half in range(2):
        lanes = pl.ds(half * LANES, LANES)
        cut = slice(half * LANES, (half + 1) * LANES)
        for comp in range(2):
            rows = slice(4 * comp, 4 * comp + 4)
            ends[half, comp, 0, even] = before[rows, cut]
            ends[half, comp, 0, odd] = centre[rows, cut]
            ends[half, comp, 1, even] = centre[rows, cut]
            ends[half, comp, 1, odd] = last[rows, cut]
            start, value = ends[half, comp, 0], ends[half, comp, 1]
            lifted[half, pl.ds(128 * comp + 15, 8, stride=16), :] = value
            for index in range(14, -1, -1):
                value = (
                    saved[2 + comp, index, :, lanes]
                    + saved[0, index, :, lanes] * start
                    + saved[1, index, :, lanes] * value
                )
                lifted[half, pl.ds(128 * comp + index, 8, stride=16), :] = value
    for block in range(4):
        for half in range(2):
            lanes = pl.ds(half * LANES, LANES)
            for comp in range(2):

                def one(index):
                    rows = pl.ds(32 * index + 8 * block, 8)
                    k = cond[rows, lanes]
                    m = 1.0 + loss[rows, lanes] if comp == 0 else jnp.ones_like(k)
                    r = lifted[half, pl.ds(128 * comp + 32 * index + 8 * block, 8), :]
                    zero = jnp.zeros_like(k)
                    return k + flow[rows, lanes], zero, k, m, [zero], [r]

                element = one(0)
                for index in range(1, 4):
                    element, a, b, c = joined(element, one(index))
                    for place, value in enumerate((a, b, *c)):
                        kept[4 * comp + block, index - 1, place, :, lanes] = value
                up, mp, low, m, rp, r = element
                for place, value in enumerate((up, mp, low, m, *rp, *r)):
                    sent[4 * comp + block, half, place] = value


def tree(elements, first, last, keep):
    if last - first == 1:
        return elements(first)
    centre = (first + last) // 2
    left, right = tree(elements, first, centre, keep), tree(elements, centre, last, keep)
    whole, a, b, c = joined(left, right)
    keep(centre - 1, a, b, c)
    return whole


def untree(kept, first, last, before, value, give):
    if last - first == 1:
        return
    centre = (first + last) // 2
    a, b, c = kept(centre - 1)
    middle = c + a * before + b * value
    give(centre - 1, middle)
    untree(kept, first, centre, before, middle, give)
    untree(kept, centre, last, middle, value, give)


def element_at(ref, *index):
    up, mp, low, m, rp, r = (ref[(*index, pl.ds(4 * place, 4))] for place in range(6))
    return up, mp, low, m, [rp], [r]


def listed(element):
    up, mp, low, m, rp, r = element
    return up, mp, low, m, *rp, *r


def pair_forward(received, sent, kept):
    targets = places(JOIN_ORDER)
    core = lax.axis_index("tun") % 2

    def one(which, group, half):
        up, mp, low, m, rp, r = (received[which, group, half, place] for place in range(6))
        return up, mp, low, m, [rp], [r]

    for group in range(8):
        for half in range(2):
            _, a, b, c = joined(one(0, group, half), one(1, group, half))
            kept[group, half, 0], kept[group, half, 1], kept[group, half, 2] = a, b, c[0]
        whole = joined(one(0, group, core), one(1, group, core))[0]
        for place, value in enumerate(listed(whole)):
            for part in range(2):
                sent[targets[2 * group + part], pl.ds(4 * place, 4)] = value[4 * part : 4 * part + 4]


def chain_forward(received, sent, kept):
    sources = places(JOIN_ORDER)

    def keep(index, a, b, c):
        kept[index, 0], kept[index, 1], kept[index, 2] = a, b, c[0]

    whole = tree(lambda index: element_at(received, sources[index]), 0, received.shape[0], keep)
    for place, value in enumerate(listed(whole)):
        for target in range(sent.shape[0]):
            sent[target, pl.ds(4 * place, 4)] = value


def chain_back(received, kept, sent, bound):
    groups, chips = received.shape[0], sent.shape[0] // 2
    sources, targets = places(FAR_ORDER), places(BACK_ORDER)
    top = {}

    def keep(index, a, b, c):
        top[index] = a, b, c[0]

    def give(index, value):
        bound[index + 1] = value

    up, mp, low, m, rp, r = tree(lambda index: element_at(received, sources[index]), 0, groups, keep)
    zero = jnp.zeros_like(up)
    value = r[0] / (low + m)
    bound[0] = zero
    give(groups - 1, value)
    untree(lambda index: top[index], 0, groups, zero, value, give)
    mine = lax.axis_index("tun") // (2 * chips)
    before, value = bound[mine], bound[mine + 1]

    def end(index, value):
        for core in range(2):
            sent[targets[2 * index + core], 4:8] = value
            if index + 1 < chips:
                sent[targets[2 * index + 2 + core], 0:4] = value

    for core in range(2):
        sent[targets[core], 0:4] = before
    end(chips - 1, value)
    untree(lambda index: [kept[index, place] for place in range(3)], 0, chips, before, value, end)


def split(value):
    high = value.astype(jnp.bfloat16)
    return high, (value - high.astype(F32)).astype(jnp.bfloat16)


def tunnel_back(received, paired, kept, high, low, face, out, carried, solved, top_matrix, rest_matrix, done):
    @pl.when(early())
    def _():
        top_matrix[...], rest_matrix[...] = high[...], low[...]

    @pl.when(jnp.logical_not(early()))
    def _():
        width_inverse(face, top_matrix, rest_matrix)

    sources = places(BACK_ORDER)
    first = lax.axis_index("tun") % 2 == 0
    for group in range(8):
        comp, block = group // 4, group % 4
        for half in range(2):
            lanes = pl.ds(half * LANES, LANES)
            parts = [sources[4 * group + 2 * part + half] for part in range(2)]
            before, value = (
                jnp.concatenate([received[part, pl.ds(start, 4)] for part in parts], axis=0) for start in (0, 4)
            )
            a, b, c = (paired[group, half, place] for place in range(3))
            centre = c + a * before + b * value
            before, value = jnp.where(first, before, centre), jnp.where(first, centre, value)
            for index in range(3, -1, -1):
                if index < 3:
                    a, b, c = (kept[group, index, place, :, lanes] for place in range(3))
                    value = c + a * before + b * value
                carried[pl.ds(128 * comp + 32 * index + 8 * block, 8), lanes] = value

    def times(one, two):
        return jnp.dot(one, two[...], preferred_element_type=F32)

    top, rest = split(carried[...])
    both = times(jnp.concatenate([top, rest], axis=0), top_matrix)
    solved[...] = both[:256] + (times(top, rest_matrix) + both[256:])
    copies = []
    for part in range(4):
        rows = pl.ds(64 * part, 64)
        copy = pltpu.make_async_copy(solved.at[rows, :], out.at[rows, :], done.at[part])
        copy.start()
        copies.append(copy)
    for copy in copies:
        copy.wait()


def width_inverse(face, high, low_part):
    count = 256
    step = 1

    def filled(start):
        parts = [face[start + LANES * half : start + LANES * (half + 1)] for half in range(2)]
        return jnp.concatenate([jnp.transpose(jnp.broadcast_to(part.reshape(1, LANES), (LANES, LANES))) for part in parts], axis=0)

    lower, upper = filled(0), filled(1)
    row = lax.broadcasted_iota(jnp.int32, (count, LANES), 0)
    one = jnp.ones((count, LANES), F32)
    m = one + jnp.where(row == 0, lower, 0.0) + jnp.where(row == count - 1, upper, 0.0)
    low, up = jnp.where(row == 0, 0.0, lower), jnp.where(row == count - 1, 0.0, upper)
    column = lax.broadcasted_iota(jnp.int32, (count, LANES), 1)
    rights = [jnp.where(row == column + LANES * half, 1.0, 0.0) for half in range(2)]

    def earlier(value, step):
        return jnp.concatenate([jnp.zeros_like(value[:step]), value[:-step]], axis=0)

    def later(value, step):
        return jnp.concatenate([value[step:], jnp.zeros_like(value[:step])], axis=0)

    while step < count:
        inverse = 1.0 / (low + m + up)
        part = m * inverse
        scaled = [right * inverse for right in rights]
        rights = [
            right + low * earlier(value, step) + up * later(value, step) for right, value in zip(rights, scaled)
        ]
        m, low, up = (
            m + low * earlier(part, step) + up * later(part, step),
            low * earlier(low * inverse, step),
            up * later(up * inverse, step),
        )
        step *= 2
    for half in range(2):
        lanes = pl.ds(half * LANES, LANES)
        top, rest = split(rights[half] / m)
        high[:, lanes] = top
        low_part[:, lanes] = rest


def call(kernel, outs, scratch, *args, place=pltpu.VMEM, out_place=pltpu.VMEM):
    if place is pltpu.HBM:
        args = [pltpu.with_memory_space_constraint(arg, place) for arg in args]
    return pl.pallas_call(
        kernel,
        out_shape=[jax.ShapeDtypeStruct(shape, dtype) for shape, dtype in outs],
        in_specs=[pl.BlockSpec(memory_space=place)] * len(args),
        out_specs=[pl.BlockSpec(memory_space=out_place)] * len(outs),
        scratch_shapes=scratch,
        compiler_params=pltpu.CompilerParams(vmem_limit_bytes=16 * 2**20),
    )(*args)


def room(*shape):
    return pltpu.VMEM(shape, F32)


def per_device(cotangent, tun_cond, tun_flow, heat_loss, hgt_cond, hgt_lift, wid_cond):
    chips, members = len(JOIN_ORDER), len(BACK_ORDER)
    count = lax.axis_size("tun")
    cores = [[first, first + 1] for first in range(0, count, 2)]
    join = [[first + 2 * chip + core for chip in JOIN_ORDER] for first in range(0, count, members) for core in range(2)]
    back = [[first + member for member in BACK_ORDER] for first in range(0, count, members)]
    far = [[first + members * group for group in FAR_ORDER] for first in range(members)]
    groups = len(FAR_ORDER)

    def exchanged(value, axis, groups=None):
        return lax.all_to_all(value, axis, 0, 0, tiled=True, axis_index_groups=groups)

    def rows(value):
        return value.reshape(-1, 256)

    elements, saved, middle, high, low, face = call(
        front,
        [((4, 32, 256), F32), ((4, 15, 8, 256), F32), ((16, 256), F32), *[((256, 256), jnp.bfloat16)] * 2, ((257,), F32)],
        [
            room(2, 8, 8, LANES),
            room(2, 256, LANES),
            room(2, 128, LANES),
            room(2, 128, LANES),
            pltpu.SemaphoreType.DMA((7,)),
        ],
        rows(cotangent),
        rows(hgt_cond),
        rows(hgt_lift),
        wid_cond,
        place=pltpu.HBM,
    )
    elements = exchanged(elements, "hgt", [list(HEIGHT_ORDER)])
    sent, kept = call(
        height_back,
        [((8, 2, 6, 8, LANES), F32), ((8, 3, 3, 8, 256), F32)],
        [room(5, 8, 256), room(2, 2, 2, 8, LANES), room(2, 256, LANES)],
        elements,
        saved,
        middle,
        rows(tun_cond),
        rows(tun_flow),
        rows(heat_loss),
    )
    received = lax.all_gather(sent, "tun", axis_index_groups=cores)
    sent, paired = call(
        pair_forward, [((chips, 24, LANES), F32), ((8, 2, 3, 8, LANES), F32)], [], received
    )
    received = exchanged(sent, "tun", join)
    sent, chain = call(
        chain_forward, [((groups, 24, LANES), F32), ((chips - 1, 3, 4, LANES), F32)], [], received
    )
    received = exchanged(sent, "tun", far)
    [sent] = call(chain_back, [((members, 8, LANES), F32)], [room(groups + 1, 4, LANES)], received, chain)
    received = exchanged(sent, "tun", back)
    [solved] = call(
        tunnel_back,
        [((256, 256), F32)],
        [
            room(256, 256),
            room(256, 256),
            pltpu.VMEM((256, 256), jnp.bfloat16),
            pltpu.VMEM((256, 256), jnp.bfloat16),
            pltpu.SemaphoreType.DMA((4,)),
        ],
        received,
        paired,
        kept,
        high,
        low,
        face,
        out_place=pltpu.HBM,
    )
    return solved.reshape(cotangent.shape)


def solution(mesh):
    in_specs = (
        P(None, "tun", "hgt", None),
        P("tun", "hgt", None),
        P("tun", "hgt", None),
        P("tun", "hgt", None),
        P("tun", "hgt", None),
        P("tun", "hgt", None),
        P(),
    )
    out_specs = P(None, "tun", "hgt", None)
    return jax.shard_map(
        per_device, mesh=mesh, in_specs=in_specs, out_specs=out_specs, check_vma=False
    )
```

```python
import jax
import jax.numpy as jnp
from jax import lax
from jax.experimental import pallas as pl
from jax.experimental.pallas import tpu as pltpu
from jax.sharding import PartitionSpec as P

F32 = jnp.float32
LANES = 128
EARLY_LAYERS = 6

HEIGHT_ORDER = (2, 3, 0, 1)
JOIN_ORDER = (10, 6, 9, 11, 14, 5, 7, 13, 15, 1, 2, 3, 0, 4, 8, 12)
FAR_ORDER = (2, 3, 0, 1)
BACK_ORDER = (21, 22, 23, 24, 25, 26, 27, 28, 29, 30, 31, 0, 1, 2, 3, 4, 5, 6, 7, 8, 9, 10, 11, 12, 13, 14, 15, 16, 17, 18, 19, 20)


def places(order):
    return [order.index(member) for member in range(len(order))]


def joined(element, following):
    up, mp, low, m, rp, r = element
    next_up, next_mp, next_low, next_m, next_rp, next_r = following
    mid = m + next_mp
    inverse = 1.0 / (mid + low + next_up)
    a, b, mid = low * inverse, next_up * inverse, mid * inverse
    c = [(one + two) * inverse for one, two in zip(r, next_rp)]
    whole = (
        up * b,
        mp + up * mid,
        next_low * a,
        next_m + next_low * mid,
        [one + up * two for one, two in zip(rp, c)],
        [one + next_low * two for one, two in zip(next_r, c)],
    )
    return whole, a, b, c


def early():
    return lax.axis_index("tun") // 8 < EARLY_LAYERS


def front(field, cond, lift, wide, elements, saved, middle, high, rest, face, pieces, fields, conds, lifts, done):
    face_copy = pltpu.make_async_copy(wide, face, done.at[6])
    face_copy.start()
    copies = []
    for source, target in ((field, fields), (cond, conds), (lift, lifts)):
        for half in range(2):
            copy = pltpu.make_async_copy(
                source.at[:, pl.ds(half * LANES, LANES)], target.at[half], done.at[len(copies)]
            )
            copy.start()
            copies.append(copy)
    face_copy.wait()

    @pl.when(early())
    def _():
        width_inverse(face, high, rest)

    for copy in copies:
        copy.wait()
    height_forward(elements, saved, middle, pieces, fields, conds, lifts)


def height_forward(elements, saved, middle, pieces, fields, conds, lifts):
    lower = [pl.ds(0, 4, stride=2), pl.ds(1, 4, stride=2)]
    for half in range(2):
        lanes = pl.ds(half * LANES, LANES)


        def cell(ref, index, base=0):
            return ref[half, pl.ds(base + index, 8, stride=16), :]

        def one(index):
            k = cell(conds, index)
            return (
                k + cell(lifts, index),
                jnp.zeros_like(k),
                k,
                jnp.ones_like(k),
                [jnp.zeros_like(k)] * 2,
                [cell(fields, index), cell(fields, index, 128)],
            )

        element = one(0)
        for index in range(1, 16):
            element, a, b, c = joined(element, one(index))
            for place, part in enumerate((a, b, *c)):
                saved[place, index - 1, :, lanes] = part
        up, mp, low, m, rp, r = element
        for place, part in enumerate((up, mp, low, m, *rp, *r)):
            pieces[half, place] = part

        def sub(which):
            up, mp, low, m, rp0, rp1, r0, r1 = (pieces[half, place, lower[which]] for place in range(8))
            return up, mp, low, m, [rp0, rp1], [r0, r1]

        whole, a, b, c = joined(sub(0), sub(1))
        for place, part in enumerate((a, b, *c)):
            middle[pl.ds(4 * place, 4), lanes] = part
        up, mp, low, m, rp, r = whole
        for place, part in enumerate((up, mp, low, m, *rp, *r)):
            for target in range(4):
                elements[target, pl.ds(4 * place, 4), lanes] = part


def height_back(elements, saved, middle, cond, flow, loss, sent, kept, bound, ends, lifted):
    def part(source, place, rows=4):
        return elements[heights[source], pl.ds(4 * place, rows), :]

    rows_of, heights = [], places(HEIGHT_ORDER)
    for source in range(4):
        low, m, r = part(source, 2), part(source, 3), part(source, 6, 8)
        if source == 0:
            low, m = jnp.zeros_like(low), m + low
        up = jnp.zeros_like(low)
        if source < 3:
            up, m, r = part(source + 1, 0), m + part(source + 1, 1), r + part(source + 1, 4, 8)
        rows_of.append([low, m, up, r])

    def twice(value):
        return jnp.concatenate([value, value], axis=0)

    scale = []
    for source in range(4):
        low, m, up, r = rows_of[source]
        inverse = 1.0 / (m + up)
        scale.append((twice(up * inverse), r * twice(inverse)))
        if source < 3:
            after = rows_of[source + 1]
            after[1] = after[1] + after[0] * (m * inverse)
            after[3] = after[3] + twice(after[0]) * scale[source][1]
    bound[0] = jnp.zeros_like(bound[0])
    value = scale[3][1]
    bound[4] = value
    for source in (2, 1, 0):
        value = scale[source][1] + scale[source][0] * value
        bound[source + 1] = value
    mine = lax.axis_index("hgt")
    before, last = bound[mine], bound[mine + 1]
    a, b, c = middle[0:4, :], middle[4:8, :], middle[8:16, :]
    centre = c + twice(a) * before + twice(b) * last
    even, odd = pl.ds(0, 4, stride=2), pl.ds(1, 4, stride=2)
    for half in range(2):
        lanes = pl.ds(half * LANES, LANES)
        cut = slice(half * LANES, (half + 1) * LANES)
        for comp in range(2):
            rows = slice(4 * comp, 4 * comp + 4)
            ends[half, comp, 0, even] = before[rows, cut]
            ends[half, comp, 0, odd] = centre[rows, cut]
            ends[half, comp, 1, even] = centre[rows, cut]
            ends[half, comp, 1, odd] = last[rows, cut]
            start, value = ends[half, comp, 0], ends[half, comp, 1]
            lifted[half, pl.ds(128 * comp + 15, 8, stride=16), :] = value
            for index in range(14, -1, -1):
                value = (
                    saved[2 + comp, index, :, lanes]
                    + saved[0, index, :, lanes] * start
                    + saved[1, index, :, lanes] * value
                )
                lifted[half, pl.ds(128 * comp + index, 8, stride=16), :] = value
    for block in range(4):
        for half in range(2):
            lanes = pl.ds(half * LANES, LANES)
            for comp in range(2):

                def one(index):
                    rows = pl.ds(32 * index + 8 * block, 8)
                    k = cond[rows, lanes]
                    m = 1.0 + loss[rows, lanes] if comp == 0 else jnp.ones_like(k)
                    r = lifted[half, pl.ds(128 * comp + 32 * index + 8 * block, 8), :]
                    zero = jnp.zeros_like(k)
                    return k + flow[rows, lanes], zero, k, m, [zero], [r]

                element = one(0)
                for index in range(1, 4):
                    element, a, b, c = joined(element, one(index))
                    for place, value in enumerate((a, b, *c)):
                        kept[4 * comp + block, index - 1, place, :, lanes] = value
                up, mp, low, m, rp, r = element
                for place, value in enumerate((up, mp, low, m, *rp, *r)):
                    sent[4 * comp + block, half, place] = value


def tree(elements, first, last, keep):
    if last - first == 1:
        return elements(first)
    centre = (first + last) // 2
    left, right = tree(elements, first, centre, keep), tree(elements, centre, last, keep)
    whole, a, b, c = joined(left, right)
    keep(centre - 1, a, b, c)
    return whole


def untree(kept, first, last, before, value, give):
    if last - first == 1:
        return
    centre = (first + last) // 2
    a, b, c = kept(centre - 1)
    middle = c + a * before + b * value
    give(centre - 1, middle)
    untree(kept, first, centre, before, middle, give)
    untree(kept, centre, last, middle, value, give)


def element_at(ref, *index):
    up, mp, low, m, rp, r = (ref[(*index, pl.ds(4 * place, 4))] for place in range(6))
    return up, mp, low, m, [rp], [r]


def listed(element):
    up, mp, low, m, rp, r = element
    return up, mp, low, m, *rp, *r


def pair_forward(received, sent, kept):
    targets = places(JOIN_ORDER)
    core = lax.axis_index("tun") % 2

    def one(which, group, half):
        up, mp, low, m, rp, r = (received[which, group, half, place] for place in range(6))
        return up, mp, low, m, [rp], [r]

    for group in range(8):
        for half in range(2):
            _, a, b, c = joined(one(0, group, half), one(1, group, half))
            kept[group, half, 0], kept[group, half, 1], kept[group, half, 2] = a, b, c[0]
        whole = joined(one(0, group, core), one(1, group, core))[0]
        for place, value in enumerate(listed(whole)):
            for part in range(2):
                sent[targets[2 * group + part], pl.ds(4 * place, 4)] = value[4 * part : 4 * part + 4]


def chain_forward(received, sent, kept):
    sources = places(JOIN_ORDER)

    def keep(index, a, b, c):
        kept[index, 0], kept[index, 1], kept[index, 2] = a, b, c[0]

    whole = tree(lambda index: element_at(received, sources[index]), 0, received.shape[0], keep)
    for place, value in enumerate(listed(whole)):
        for target in range(sent.shape[0]):
            sent[target, pl.ds(4 * place, 4)] = value


def chain_back(received, kept, sent, bound):
    groups, chips = received.shape[0], sent.shape[0] // 2
    sources, targets = places(FAR_ORDER), places(BACK_ORDER)
    top = {}

    def keep(index, a, b, c):
        top[index] = a, b, c[0]

    def give(index, value):
        bound[index + 1] = value

    up, mp, low, m, rp, r = tree(lambda index: element_at(received, sources[index]), 0, groups, keep)
    zero = jnp.zeros_like(up)
    value = r[0] / (low + m)
    bound[0] = zero
    give(groups - 1, value)
    untree(lambda index: top[index], 0, groups, zero, value, give)
    mine = lax.axis_index("tun") // (2 * chips)
    before, value = bound[mine], bound[mine + 1]

    def end(index, value):
        for core in range(2):
            sent[targets[2 * index + core], 4:8] = value
            if index + 1 < chips:
                sent[targets[2 * index + 2 + core], 0:4] = value

    for core in range(2):
        sent[targets[core], 0:4] = before
    end(chips - 1, value)
    untree(lambda index: [kept[index, place] for place in range(3)], 0, chips, before, value, end)


def split(value):
    high = value.astype(jnp.bfloat16)
    return high, (value - high.astype(F32)).astype(jnp.bfloat16)


def tunnel_back(received, paired, kept, high, low, face, out, carried, solved, top_matrix, rest_matrix, done):
    @pl.when(early())
    def _():
        top_matrix[...], rest_matrix[...] = high[...], low[...]

    @pl.when(jnp.logical_not(early()))
    def _():
        width_inverse(face, top_matrix, rest_matrix)

    sources = places(BACK_ORDER)
    first = lax.axis_index("tun") % 2 == 0
    for group in range(8):
        comp, block = group // 4, group % 4
        for half in range(2):
            lanes = pl.ds(half * LANES, LANES)
            parts = [sources[4 * group + 2 * part + half] for part in range(2)]
            before, value = (
                jnp.concatenate([received[part, pl.ds(start, 4)] for part in parts], axis=0) for start in (0, 4)
            )
            a, b, c = (paired[group, half, place] for place in range(3))
            centre = c + a * before + b * value
            before, value = jnp.where(first, before, centre), jnp.where(first, centre, value)
            for index in range(3, -1, -1):
                if index < 3:
                    a, b, c = (kept[group, index, place, :, lanes] for place in range(3))
                    value = c + a * before + b * value
                carried[pl.ds(128 * comp + 32 * index + 8 * block, 8), lanes] = value

    def times(one, two):
        return jnp.dot(one, two[...], preferred_element_type=F32)

    top, rest = split(carried[...])
    both = times(jnp.concatenate([top, rest], axis=0), top_matrix)
    solved[...] = both[:256] + (times(top, rest_matrix) + both[256:])
    copies = []
    for part in range(4):
        rows = pl.ds(64 * part, 64)
        copy = pltpu.make_async_copy(solved.at[rows, :], out.at[rows, :], done.at[part])
        copy.start()
        copies.append(copy)
    for copy in copies:
        copy.wait()


def width_inverse(face, high, low_part):
    count = 256
    step = 1

    def filled(start):
        parts = [face[start + LANES * half : start + LANES * (half + 1)] for half in range(2)]
        return jnp.concatenate([jnp.transpose(jnp.broadcast_to(part.reshape(1, LANES), (LANES, LANES))) for part in parts], axis=0)

    lower, upper = filled(0), filled(1)
    row = lax.broadcasted_iota(jnp.int32, (count, LANES), 0)
    one = jnp.ones((count, LANES), F32)
    m = one + jnp.where(row == 0, lower, 0.0) + jnp.where(row == count - 1, upper, 0.0)
    low, up = jnp.where(row == 0, 0.0, lower), jnp.where(row == count - 1, 0.0, upper)
    column = lax.broadcasted_iota(jnp.int32, (count, LANES), 1)
    rights = [jnp.where(row == column + LANES * half, 1.0, 0.0) for half in range(2)]

    def earlier(value, step):
        return jnp.concatenate([jnp.zeros_like(value[:step]), value[:-step]], axis=0)

    def later(value, step):
        return jnp.concatenate([value[step:], jnp.zeros_like(value[:step])], axis=0)

    while step < count:
        inverse = 1.0 / (low + m + up)
        part = m * inverse
        scaled = [right * inverse for right in rights]
        rights = [
            right + low * earlier(value, step) + up * later(value, step) for right, value in zip(rights, scaled)
        ]
        m, low, up = (
            m + low * earlier(part, step) + up * later(part, step),
            low * earlier(low * inverse, step),
            up * later(up * inverse, step),
        )
        step *= 2
    for half in range(2):
        lanes = pl.ds(half * LANES, LANES)
        top, rest = split(rights[half] / m)
        high[:, lanes] = top
        low_part[:, lanes] = rest


def call(kernel, outs, scratch, *args, place=pltpu.VMEM, out_place=pltpu.VMEM):
    if place is pltpu.HBM:
        args = [pltpu.with_memory_space_constraint(arg, place) for arg in args]
    return pl.pallas_call(
        kernel,
        out_shape=[jax.ShapeDtypeStruct(shape, dtype) for shape, dtype in outs],
        in_specs=[pl.BlockSpec(memory_space=place)] * len(args),
        out_specs=[pl.BlockSpec(memory_space=out_place)] * len(outs),
        scratch_shapes=scratch,
        compiler_params=pltpu.CompilerParams(vmem_limit_bytes=16 * 2**20),
    )(*args)


def room(*shape):
    return pltpu.VMEM(shape, F32)


def per_device(cotangent, tun_cond, tun_flow, heat_loss, hgt_cond, hgt_lift, wid_cond):
    chips, members = len(JOIN_ORDER), len(BACK_ORDER)
    count = lax.axis_size("tun")
    cores = [[first, first + 1] for first in range(0, count, 2)]
    join = [[first + 2 * chip + core for chip in JOIN_ORDER] for first in range(0, count, members) for core in range(2)]
    back = [[first + member for member in BACK_ORDER] for first in range(0, count, members)]
    far = [[first + members * group for group in FAR_ORDER] for first in range(members)]
    groups = len(FAR_ORDER)

    def exchanged(value, axis, groups=None):
        return lax.all_to_all(value, axis, 0, 0, tiled=True, axis_index_groups=groups)

    def rows(value):
        return value.reshape(-1, 256)

    elements, saved, middle, high, low, face = call(
        front,
        [((4, 32, 256), F32), ((4, 15, 8, 256), F32), ((16, 256), F32), *[((256, 256), jnp.bfloat16)] * 2, ((257,), F32)],
        [
            room(2, 8, 8, LANES),
            room(2, 256, LANES),
            room(2, 128, LANES),
            room(2, 128, LANES),
            pltpu.SemaphoreType.DMA((7,)),
        ],
        rows(cotangent),
        rows(hgt_cond),
        rows(hgt_lift),
        wid_cond,
        place=pltpu.HBM,
    )
    elements = exchanged(elements, "hgt", [list(HEIGHT_ORDER)])
    sent, kept = call(
        height_back,
        [((8, 2, 6, 8, LANES), F32), ((8, 3, 3, 8, 256), F32)],
        [room(5, 8, 256), room(2, 2, 2, 8, LANES), room(2, 256, LANES)],
        elements,
        saved,
        middle,
        rows(tun_cond),
        rows(tun_flow),
        rows(heat_loss),
    )
    received = lax.all_gather(sent, "tun", axis_index_groups=cores)
    sent, paired = call(
        pair_forward, [((chips, 24, LANES), F32), ((8, 2, 3, 8, LANES), F32)], [], received
    )
    received = exchanged(sent, "tun", join)
    sent, chain = call(
        chain_forward, [((groups, 24, LANES), F32), ((chips - 1, 3, 4, LANES), F32)], [], received
    )
    received = exchanged(sent, "tun", far)
    [sent] = call(chain_back, [((members, 8, LANES), F32)], [room(groups + 1, 4, LANES)], received, chain)
    received = exchanged(sent, "tun", back)
    [solved] = call(
        tunnel_back,
        [((256, 256), F32)],
        [
            room(256, 256),
            room(256, 256),
            pltpu.VMEM((256, 256), jnp.bfloat16),
            pltpu.VMEM((256, 256), jnp.bfloat16),
            pltpu.SemaphoreType.DMA((4,)),
        ],
        received,
        paired,
        kept,
        high,
        low,
        face,
        out_place=pltpu.HBM,
    )
    return solved.reshape(cotangent.shape)


def solution(mesh):
    in_specs = (
        P(None, "tun", "hgt", None),
        P("tun", "hgt", None),
        P("tun", "hgt", None),
        P("tun", "hgt", None),
        P("tun", "hgt", None),
        P("tun", "hgt", None),
        P(),
    )
    out_specs = P(None, "tun", "hgt", None)
    return jax.shard_map(
        per_device, mesh=mesh, in_specs=in_specs, out_specs=out_specs, check_vma=False
    )
```

```python
import jax
import jax.numpy as jnp
from jax import lax
from jax.experimental import pallas as pl
from jax.experimental.pallas import tpu as pltpu
from jax.sharding import PartitionSpec as P

F32 = jnp.float32
LANES = 128
EARLY_LAYERS = 6

HEIGHT_ORDER = (2, 3, 0, 1)
JOIN_ORDER = (10, 6, 9, 11, 14, 5, 7, 13, 15, 1, 2, 3, 0, 4, 8, 12)
FAR_ORDER = (2, 3, 0, 1)
BACK_ORDER = (21, 22, 23, 24, 25, 26, 27, 28, 29, 30, 31, 0, 1, 2, 3, 4, 5, 6, 7, 8, 9, 10, 11, 12, 13, 14, 15, 16, 17, 18, 19, 20)


def places(order):
    return [order.index(member) for member in range(len(order))]


def joined(element, following):
    up, mp, low, m, rp, r = element
    next_up, next_mp, next_low, next_m, next_rp, next_r = following
    mid = m + next_mp
    inverse = 1.0 / (mid + low + next_up)
    a, b, mid = low * inverse, next_up * inverse, mid * inverse
    c = [(one + two) * inverse for one, two in zip(r, next_rp)]
    whole = (
        up * b,
        mp + up * mid,
        next_low * a,
        next_m + next_low * mid,
        [one + up * two for one, two in zip(rp, c)],
        [one + next_low * two for one, two in zip(next_r, c)],
    )
    return whole, a, b, c


def early():
    return lax.axis_index("tun") // 8 < EARLY_LAYERS


def front(field, cond, lift, wide, elements, saved, middle, high, rest, face, pieces, fields, conds, lifts, done):
    face_copy = pltpu.make_async_copy(wide, face, done.at[6])
    face_copy.start()
    copies = []
    for source, target in ((field, fields), (cond, conds), (lift, lifts)):
        for half in range(2):
            copy = pltpu.make_async_copy(
                source.at[:, pl.ds(half * LANES, LANES)], target.at[half], done.at[len(copies)]
            )
            copy.start()
            copies.append(copy)
    face_copy.wait()

    @pl.when(early())
    def _():
        width_inverse(face, high, rest)

    for copy in copies:
        copy.wait()
    height_forward(elements, saved, middle, pieces, fields, conds, lifts)


def height_forward(elements, saved, middle, pieces, fields, conds, lifts):
    lower = [pl.ds(0, 4, stride=2), pl.ds(1, 4, stride=2)]
    for half in range(2):
        lanes = pl.ds(half * LANES, LANES)


        def cell(ref, index, base=0):
            return ref[half, pl.ds(base + index, 8, stride=16), :]

        def one(index):
            k = cell(conds, index)
            return (
                k + cell(lifts, index),
                jnp.zeros_like(k),
                k,
                jnp.ones_like(k),
                [jnp.zeros_like(k)] * 2,
                [cell(fields, index), cell(fields, index, 128)],
            )

        element = one(0)
        for index in range(1, 16):
            element, a, b, c = joined(element, one(index))
            for place, part in enumerate((a, b, *c)):
                saved[place, index - 1, :, lanes] = part
        up, mp, low, m, rp, r = element
        for place, part in enumerate((up, mp, low, m, *rp, *r)):
            pieces[half, place] = part

        def sub(which):
            up, mp, low, m, rp0, rp1, r0, r1 = (pieces[half, place, lower[which]] for place in range(8))
            return up, mp, low, m, [rp0, rp1], [r0, r1]

        whole, a, b, c = joined(sub(0), sub(1))
        for place, part in enumerate((a, b, *c)):
            middle[pl.ds(4 * place, 4), lanes] = part
        up, mp, low, m, rp, r = whole
        for place, part in enumerate((up, mp, low, m, *rp, *r)):
            for target in range(4):
                elements[target, pl.ds(4 * place, 4), lanes] = part


def height_back(elements, saved, middle, cond, flow, loss, sent, kept, bound, ends, lifted):
    def part(source, place, rows=4):
        return elements[heights[source], pl.ds(4 * place, rows), :]

    rows_of, heights = [], places(HEIGHT_ORDER)
    for source in range(4):
        low, m, r = part(source, 2), part(source, 3), part(source, 6, 8)
        if source == 0:
            low, m = jnp.zeros_like(low), m + low
        up = jnp.zeros_like(low)
        if source < 3:
            up, m, r = part(source + 1, 0), m + part(source + 1, 1), r + part(source + 1, 4, 8)
        rows_of.append([low, m, up, r])

    def twice(value):
        return jnp.concatenate([value, value], axis=0)

    scale = []
    for source in range(4):
        low, m, up, r = rows_of[source]
        inverse = 1.0 / (m + up)
        scale.append((twice(up * inverse), r * twice(inverse)))
        if source < 3:
            after = rows_of[source + 1]
            after[1] = after[1] + after[0] * (m * inverse)
            after[3] = after[3] + twice(after[0]) * scale[source][1]
    bound[0] = jnp.zeros_like(bound[0])
    value = scale[3][1]
    bound[4] = value
    for source in (2, 1, 0):
        value = scale[source][1] + scale[source][0] * value
        bound[source + 1] = value
    mine = lax.axis_index("hgt")
    before, last = bound[mine], bound[mine + 1]
    a, b, c = middle[0:4, :], middle[4:8, :], middle[8:16, :]
    centre = c + twice(a) * before + twice(b) * last
    even, odd = pl.ds(0, 4, stride=2), pl.ds(1, 4, stride=2)
    for half in range(2):
        lanes = pl.ds(half * LANES, LANES)
        cut = slice(half * LANES, (half + 1) * LANES)
        for comp in range(2):
            rows = slice(4 * comp, 4 * comp + 4)
            ends[half, comp, 0, even] = before[rows, cut]
            ends[half, comp, 0, odd] = centre[rows, cut]
            ends[half, comp, 1, even] = centre[rows, cut]
            ends[half, comp, 1, odd] = last[rows, cut]
            start, value = ends[half, comp, 0], ends[half, comp, 1]
            lifted[half, pl.ds(128 * comp + 15, 8, stride=16), :] = value
            for index in range(14, -1, -1):
                value = (
                    saved[2 + comp, index, :, lanes]
                    + saved[0, index, :, lanes] * start
                    + saved[1, index, :, lanes] * value
                )
                lifted[half, pl.ds(128 * comp + index, 8, stride=16), :] = value
    for block in range(4):
        for half in range(2):
            lanes = pl.ds(half * LANES, LANES)
            for comp in range(2):

                def one(index):
                    rows = pl.ds(32 * index + 8 * block, 8)
                    k = cond[rows, lanes]
                    m = 1.0 + loss[rows, lanes] if comp == 0 else jnp.ones_like(k)
                    r = lifted[half, pl.ds(128 * comp + 32 * index + 8 * block, 8), :]
                    zero = jnp.zeros_like(k)
                    return k + flow[rows, lanes], zero, k, m, [zero], [r]

                element = one(0)
                for index in range(1, 4):
                    element, a, b, c = joined(element, one(index))
                    for place, value in enumerate((a, b, *c)):
                        kept[4 * comp + block, index - 1, place, :, lanes] = value
                up, mp, low, m, rp, r = element
                for place, value in enumerate((up, mp, low, m, *rp, *r)):
                    sent[4 * comp + block, half, place] = value


def tree(elements, first, last, keep):
    if last - first == 1:
        return elements(first)
    centre = (first + last) // 2
    left, right = tree(elements, first, centre, keep), tree(elements, centre, last, keep)
    whole, a, b, c = joined(left, right)
    keep(centre - 1, a, b, c)
    return whole


def untree(kept, first, last, before, value, give):
    if last - first == 1:
        return
    centre = (first + last) // 2
    a, b, c = kept(centre - 1)
    middle = c + a * before + b * value
    give(centre - 1, middle)
    untree(kept, first, centre, before, middle, give)
    untree(kept, centre, last, middle, value, give)


def element_at(ref, *index):
    up, mp, low, m, rp, r = (ref[(*index, pl.ds(4 * place, 4))] for place in range(6))
    return up, mp, low, m, [rp], [r]


def listed(element):
    up, mp, low, m, rp, r = element
    return up, mp, low, m, *rp, *r


def pair_forward(received, sent, kept):
    targets = places(JOIN_ORDER)
    core = lax.axis_index("tun") % 2

    def one(which, group, half):
        up, mp, low, m, rp, r = (received[which, group, half, place] for place in range(6))
        return up, mp, low, m, [rp], [r]

    for group in range(8):
        for half in range(2):
            _, a, b, c = joined(one(0, group, half), one(1, group, half))
            kept[group, half, 0], kept[group, half, 1], kept[group, half, 2] = a, b, c[0]
        whole = joined(one(0, group, core), one(1, group, core))[0]
        comp, block = group // 4, group % 4
        up, mp, low, m, rp, r = listed(whole)
        values = [up, mp, m, rp, r]
        for part in range(4):
            rows = slice(2 * part, 2 * part + 2)
            for place, value in enumerate(values):
                sent[targets[4 * block + part], 2 * place + comp] = value[rows]
            if comp == 0:
                sent[targets[4 * block + part], 10] = low[rows]


def chain_forward(received, sent, kept):
    sources = places(JOIN_ORDER)

    def keep(index, a, b, c):
        kept[index, 0], kept[index, 1], kept[index, 2] = a, b, c[0]

    def one(index):
        source = sources[index]
        pairs = [(received[source, 2 * place], received[source, 2 * place + 1]) for place in range(5)]
        first = received[source, 10]
        low = jnp.concatenate([first, first * (pairs[0][1] / pairs[0][0])], axis=0)
        up, mp, m, rp, r = (jnp.concatenate(pair, axis=0) for pair in pairs)
        return up, mp, low, m, [rp], [r]

    whole = tree(one, 0, received.shape[0], keep)
    for place, value in enumerate(listed(whole)):
        for target in range(sent.shape[0]):
            sent[target, pl.ds(4 * place, 4)] = value


def chain_back(received, kept, sent, bound):
    groups, chips = received.shape[0], sent.shape[0] // 2
    sources, targets = places(FAR_ORDER), places(BACK_ORDER)
    top = {}

    def keep(index, a, b, c):
        top[index] = a, b, c[0]

    def give(index, value):
        bound[index + 1] = value

    up, mp, low, m, rp, r = tree(lambda index: element_at(received, sources[index]), 0, groups, keep)
    zero = jnp.zeros_like(up)
    value = r[0] / (low + m)
    bound[0] = zero
    give(groups - 1, value)
    untree(lambda index: top[index], 0, groups, zero, value, give)
    mine = lax.axis_index("tun") // (2 * chips)
    before, value = bound[mine], bound[mine + 1]

    def end(index, value):
        for core in range(2):
            sent[targets[2 * index + core], 4:8] = value
            if index + 1 < chips:
                sent[targets[2 * index + 2 + core], 0:4] = value

    for core in range(2):
        sent[targets[core], 0:4] = before
    end(chips - 1, value)
    untree(lambda index: [kept[index, place] for place in range(3)], 0, chips, before, value, end)


def split(value):
    high = value.astype(jnp.bfloat16)
    return high, (value - high.astype(F32)).astype(jnp.bfloat16)


def tunnel_back(received, paired, kept, high, low, face, out, carried, solved, top_matrix, rest_matrix, done):
    @pl.when(early())
    def _():
        top_matrix[...], rest_matrix[...] = high[...], low[...]

    @pl.when(jnp.logical_not(early()))
    def _():
        width_inverse(face, top_matrix, rest_matrix)

    sources = places(BACK_ORDER)
    first = lax.axis_index("tun") % 2 == 0
    for group in range(8):
        comp, block = group // 4, group % 4
        for half in range(2):
            lanes = pl.ds(half * LANES, LANES)
            parts = [sources[8 * block + 2 * part + half] for part in range(4)]
            before, value = (
                jnp.concatenate([received[part, pl.ds(start + 2 * comp, 2)] for part in parts], axis=0)
                for start in (0, 4)
            )
            a, b, c = (paired[group, half, place] for place in range(3))
            centre = c + a * before + b * value
            before, value = jnp.where(first, before, centre), jnp.where(first, centre, value)
            for index in range(3, -1, -1):
                if index < 3:
                    a, b, c = (kept[group, index, place, :, lanes] for place in range(3))
                    value = c + a * before + b * value
                carried[pl.ds(128 * comp + 32 * index + 8 * block, 8), lanes] = value

    def times(one, two):
        return jnp.dot(one, two[...], preferred_element_type=F32)

    top, rest = split(carried[...])
    both = times(jnp.concatenate([top, rest], axis=0), top_matrix)
    solved[...] = both[:256] + (times(top, rest_matrix) + both[256:])
    copies = []
    for part in range(4):
        rows = pl.ds(64 * part, 64)
        copy = pltpu.make_async_copy(solved.at[rows, :], out.at[rows, :], done.at[part])
        copy.start()
        copies.append(copy)
    for copy in copies:
        copy.wait()


def width_inverse(face, high, low_part):
    count = 256
    step = 1

    def filled(start):
        parts = [face[start + LANES * half : start + LANES * (half + 1)] for half in range(2)]
        return jnp.concatenate([jnp.transpose(jnp.broadcast_to(part.reshape(1, LANES), (LANES, LANES))) for part in parts], axis=0)

    lower, upper = filled(0), filled(1)
    row = lax.broadcasted_iota(jnp.int32, (count, LANES), 0)
    one = jnp.ones((count, LANES), F32)
    m = one + jnp.where(row == 0, lower, 0.0) + jnp.where(row == count - 1, upper, 0.0)
    low, up = jnp.where(row == 0, 0.0, lower), jnp.where(row == count - 1, 0.0, upper)
    column = lax.broadcasted_iota(jnp.int32, (count, LANES), 1)
    rights = [jnp.where(row == column + LANES * half, 1.0, 0.0) for half in range(2)]

    def earlier(value, step):
        return jnp.concatenate([jnp.zeros_like(value[:step]), value[:-step]], axis=0)

    def later(value, step):
        return jnp.concatenate([value[step:], jnp.zeros_like(value[:step])], axis=0)

    while step < count:
        inverse = 1.0 / (low + m + up)
        part = m * inverse
        scaled = [right * inverse for right in rights]
        rights = [
            right + low * earlier(value, step) + up * later(value, step) for right, value in zip(rights, scaled)
        ]
        m, low, up = (
            m + low * earlier(part, step) + up * later(part, step),
            low * earlier(low * inverse, step),
            up * later(up * inverse, step),
        )
        step *= 2
    for half in range(2):
        lanes = pl.ds(half * LANES, LANES)
        top, rest = split(rights[half] / m)
        high[:, lanes] = top
        low_part[:, lanes] = rest


def call(kernel, outs, scratch, *args, place=pltpu.VMEM, out_place=pltpu.VMEM):
    if place is pltpu.HBM:
        args = [pltpu.with_memory_space_constraint(arg, place) for arg in args]
    return pl.pallas_call(
        kernel,
        out_shape=[jax.ShapeDtypeStruct(shape, dtype) for shape, dtype in outs],
        in_specs=[pl.BlockSpec(memory_space=place)] * len(args),
        out_specs=[pl.BlockSpec(memory_space=out_place)] * len(outs),
        scratch_shapes=scratch,
        compiler_params=pltpu.CompilerParams(vmem_limit_bytes=16 * 2**20),
    )(*args)


def room(*shape):
    return pltpu.VMEM(shape, F32)


def per_device(cotangent, tun_cond, tun_flow, heat_loss, hgt_cond, hgt_lift, wid_cond):
    chips, members = len(JOIN_ORDER), len(BACK_ORDER)
    count = lax.axis_size("tun")
    cores = [[first, first + 1] for first in range(0, count, 2)]
    join = [[first + 2 * chip + core for chip in JOIN_ORDER] for first in range(0, count, members) for core in range(2)]
    back = [[first + member for member in BACK_ORDER] for first in range(0, count, members)]
    far = [[first + members * group for group in FAR_ORDER] for first in range(members)]
    groups = len(FAR_ORDER)

    def exchanged(value, axis, groups=None):
        return lax.all_to_all(value, axis, 0, 0, tiled=True, axis_index_groups=groups)

    def rows(value):
        return value.reshape(-1, 256)

    elements, saved, middle, high, low, face = call(
        front,
        [((4, 32, 256), F32), ((4, 15, 8, 256), F32), ((16, 256), F32), *[((256, 256), jnp.bfloat16)] * 2, ((257,), F32)],
        [
            room(2, 8, 8, LANES),
            room(2, 256, LANES),
            room(2, 128, LANES),
            room(2, 128, LANES),
            pltpu.SemaphoreType.DMA((7,)),
        ],
        rows(cotangent),
        rows(hgt_cond),
        rows(hgt_lift),
        wid_cond,
        place=pltpu.HBM,
    )
    elements = exchanged(elements, "hgt", [list(HEIGHT_ORDER)])
    sent, kept = call(
        height_back,
        [((8, 2, 6, 8, LANES), F32), ((8, 3, 3, 8, 256), F32)],
        [room(5, 8, 256), room(2, 2, 2, 8, LANES), room(2, 256, LANES)],
        elements,
        saved,
        middle,
        rows(tun_cond),
        rows(tun_flow),
        rows(heat_loss),
    )
    received = lax.all_gather(sent, "tun", axis_index_groups=cores)
    sent, paired = call(
        pair_forward, [((chips, 11, 2, LANES), F32), ((8, 2, 3, 8, LANES), F32)], [], received
    )
    received = exchanged(sent, "tun", join)
    sent, chain = call(
        chain_forward, [((groups, 24, LANES), F32), ((chips - 1, 3, 4, LANES), F32)], [], received
    )
    received = exchanged(sent, "tun", far)
    [sent] = call(chain_back, [((members, 8, LANES), F32)], [room(groups + 1, 4, LANES)], received, chain)
    received = exchanged(sent, "tun", back)
    [solved] = call(
        tunnel_back,
        [((256, 256), F32)],
        [
            room(256, 256),
            room(256, 256),
            pltpu.VMEM((256, 256), jnp.bfloat16),
            pltpu.VMEM((256, 256), jnp.bfloat16),
            pltpu.SemaphoreType.DMA((4,)),
        ],
        received,
        paired,
        kept,
        high,
        low,
        face,
        out_place=pltpu.HBM,
    )
    return solved.reshape(cotangent.shape)


def solution(mesh):
    in_specs = (
        P(None, "tun", "hgt", None),
        P("tun", "hgt", None),
        P("tun", "hgt", None),
        P("tun", "hgt", None),
        P("tun", "hgt", None),
        P("tun", "hgt", None),
        P(),
    )
    out_specs = P(None, "tun", "hgt", None)
    return jax.shard_map(
        per_device, mesh=mesh, in_specs=in_specs, out_specs=out_specs, check_vma=False
    )
```

```python
import jax
import jax.numpy as jnp
from jax import lax
from jax.experimental import pallas as pl
from jax.experimental.pallas import tpu as pltpu
from jax.sharding import PartitionSpec as P

F32 = jnp.float32
LANES = 128
EARLY_LAYERS = 6

HEIGHT_ORDER = (2, 3, 0, 1)
JOIN_ORDER = (10, 6, 9, 11, 14, 5, 7, 13, 15, 1, 2, 3, 0, 4, 8, 12)
FAR_ORDER = (2, 3, 0, 1)
BACK_ORDER = (21, 22, 23, 24, 25, 26, 27, 28, 29, 30, 31, 0, 1, 2, 3, 4, 5, 6, 7, 8, 9, 10, 11, 12, 13, 14, 15, 16, 17, 18, 19, 20)


def places(order):
    return [order.index(member) for member in range(len(order))]


def joined(element, following):
    up, mp, low, m, rp, r = element
    next_up, next_mp, next_low, next_m, next_rp, next_r = following
    mid = m + next_mp
    inverse = 1.0 / (mid + low + next_up)
    a, b, mid = low * inverse, next_up * inverse, mid * inverse
    c = [(one + two) * inverse for one, two in zip(r, next_rp)]
    whole = (
        up * b,
        mp + up * mid,
        next_low * a,
        next_m + next_low * mid,
        [one + up * two for one, two in zip(rp, c)],
        [one + next_low * two for one, two in zip(next_r, c)],
    )
    return whole, a, b, c


def early():
    return lax.axis_index("tun") // 8 < EARLY_LAYERS


def front(field, cond, lift, wide, elements, saved, middle, high, rest, face, pieces, fields, conds, lifts, done):
    face_copy = pltpu.make_async_copy(wide, face, done.at[6])
    face_copy.start()
    copies = []
    for source, target in ((field, fields), (cond, conds), (lift, lifts)):
        for half in range(2):
            copy = pltpu.make_async_copy(
                source.at[:, pl.ds(half * LANES, LANES)], target.at[half], done.at[len(copies)]
            )
            copy.start()
            copies.append(copy)
    face_copy.wait()

    @pl.when(early())
    def _():
        width_inverse(face, high, rest)

    for copy in copies:
        copy.wait()
    height_forward(elements, saved, middle, pieces, fields, conds, lifts)


def height_forward(elements, saved, middle, pieces, fields, conds, lifts):
    lower = [pl.ds(0, 4, stride=2), pl.ds(1, 4, stride=2)]
    for half in range(2):
        lanes = pl.ds(half * LANES, LANES)


        def cell(ref, index, base=0):
            return ref[half, pl.ds(base + index, 8, stride=16), :]

        def one(index):
            k = cell(conds, index)
            return (
                k + cell(lifts, index),
                jnp.zeros_like(k),
                k,
                jnp.ones_like(k),
                [jnp.zeros_like(k)] * 2,
                [cell(fields, index), cell(fields, index, 128)],
            )

        def keep(index, a, b, c):
            for place, part in enumerate((a, b, *c)):
                saved[place, index, :, lanes] = part

        up, mp, low, m, rp, r = tree(one, 0, 16, keep)
        for place, part in enumerate((up, mp, low, m, *rp, *r)):
            pieces[half, place] = part

        def sub(which):
            up, mp, low, m, rp0, rp1, r0, r1 = (pieces[half, place, lower[which]] for place in range(8))
            return up, mp, low, m, [rp0, rp1], [r0, r1]

        whole, a, b, c = joined(sub(0), sub(1))
        for place, part in enumerate((a, b, *c)):
            middle[pl.ds(4 * place, 4), lanes] = part
        up, mp, low, m, rp, r = whole
        for place, part in enumerate((up, mp, low, m, *rp, *r)):
            for target in range(4):
                elements[target, pl.ds(4 * place, 4), lanes] = part


def height_back(elements, saved, middle, cond, flow, loss, sent, kept, bound, ends, lifted):
    def part(source, place, rows=4):
        return elements[heights[source], pl.ds(4 * place, rows), :]

    rows_of, heights = [], places(HEIGHT_ORDER)
    for source in range(4):
        low, m, r = part(source, 2), part(source, 3), part(source, 6, 8)
        if source == 0:
            low, m = jnp.zeros_like(low), m + low
        up = jnp.zeros_like(low)
        if source < 3:
            up, m, r = part(source + 1, 0), m + part(source + 1, 1), r + part(source + 1, 4, 8)
        rows_of.append([low, m, up, r])

    def twice(value):
        return jnp.concatenate([value, value], axis=0)

    scale = []
    for source in range(4):
        low, m, up, r = rows_of[source]
        inverse = 1.0 / (m + up)
        scale.append((twice(up * inverse), r * twice(inverse)))
        if source < 3:
            after = rows_of[source + 1]
            after[1] = after[1] + after[0] * (m * inverse)
            after[3] = after[3] + twice(after[0]) * scale[source][1]
    bound[0] = jnp.zeros_like(bound[0])
    value = scale[3][1]
    bound[4] = value
    for source in (2, 1, 0):
        value = scale[source][1] + scale[source][0] * value
        bound[source + 1] = value
    mine = lax.axis_index("hgt")
    before, last = bound[mine], bound[mine + 1]
    a, b, c = middle[0:4, :], middle[4:8, :], middle[8:16, :]
    centre = c + twice(a) * before + twice(b) * last
    even, odd = pl.ds(0, 4, stride=2), pl.ds(1, 4, stride=2)
    for half in range(2):
        lanes = pl.ds(half * LANES, LANES)
        cut = slice(half * LANES, (half + 1) * LANES)
        for comp in range(2):
            rows = slice(4 * comp, 4 * comp + 4)
            ends[half, comp, 0, even] = before[rows, cut]
            ends[half, comp, 0, odd] = centre[rows, cut]
            ends[half, comp, 1, even] = centre[rows, cut]
            ends[half, comp, 1, odd] = last[rows, cut]
            start, value = ends[half, comp, 0], ends[half, comp, 1]
            lifted[half, pl.ds(128 * comp + 15, 8, stride=16), :] = value

            def give(index, cell):
                lifted[half, pl.ds(128 * comp + index, 8, stride=16), :] = cell

            def parts(index):
                return [saved[place, index, :, lanes] for place in (0, 1, 2 + comp)]

            untree(parts, 0, 16, start, value, give)
    for block in range(4):
        for half in range(2):
            lanes = pl.ds(half * LANES, LANES)
            for comp in range(2):

                def one(index):
                    rows = pl.ds(32 * index + 8 * block, 8)
                    k = cond[rows, lanes]
                    m = 1.0 + loss[rows, lanes] if comp == 0 else jnp.ones_like(k)
                    r = lifted[half, pl.ds(128 * comp + 32 * index + 8 * block, 8), :]
                    zero = jnp.zeros_like(k)
                    return k + flow[rows, lanes], zero, k, m, [zero], [r]

                element = one(0)
                for index in range(1, 4):
                    element, a, b, c = joined(element, one(index))
                    for place, value in enumerate((a, b, *c)):
                        kept[4 * comp + block, index - 1, place, :, lanes] = value
                up, mp, low, m, rp, r = element
                for place, value in enumerate((up, mp, low, m, *rp, *r)):
                    sent[4 * comp + block, half, place] = value


def tree(elements, first, last, keep):
    if last - first == 1:
        return elements(first)
    centre = (first + last) // 2
    left, right = tree(elements, first, centre, keep), tree(elements, centre, last, keep)
    whole, a, b, c = joined(left, right)
    keep(centre - 1, a, b, c)
    return whole


def untree(kept, first, last, before, value, give):
    if last - first == 1:
        return
    centre = (first + last) // 2
    a, b, c = kept(centre - 1)
    middle = c + a * before + b * value
    give(centre - 1, middle)
    untree(kept, first, centre, before, middle, give)
    untree(kept, centre, last, middle, value, give)


def element_at(ref, *index):
    up, mp, low, m, rp, r = (ref[(*index, pl.ds(4 * place, 4))] for place in range(6))
    return up, mp, low, m, [rp], [r]


def listed(element):
    up, mp, low, m, rp, r = element
    return up, mp, low, m, *rp, *r


def pair_forward(received, sent, kept):
    targets = places(JOIN_ORDER)
    core = lax.axis_index("tun") % 2

    def one(which, group, half):
        up, mp, low, m, rp, r = (received[which, group, half, place] for place in range(6))
        return up, mp, low, m, [rp], [r]

    for group in range(8):
        for half in range(2):
            _, a, b, c = joined(one(0, group, half), one(1, group, half))
            kept[group, half, 0], kept[group, half, 1], kept[group, half, 2] = a, b, c[0]
        whole = joined(one(0, group, core), one(1, group, core))[0]
        comp, block = group // 4, group % 4
        up, mp, low, m, rp, r = listed(whole)
        values = [up, mp, m, rp, r]
        for part in range(4):
            rows = slice(2 * part, 2 * part + 2)
            for place, value in enumerate(values):
                sent[targets[4 * block + part], 2 * place + comp] = value[rows]
            if comp == 0:
                sent[targets[4 * block + part], 10] = low[rows]


def chain_forward(received, sent, kept):
    sources = places(JOIN_ORDER)

    def keep(index, a, b, c):
        kept[index, 0], kept[index, 1], kept[index, 2] = a, b, c[0]

    def one(index):
        source = sources[index]
        pairs = [(received[source, 2 * place], received[source, 2 * place + 1]) for place in range(5)]
        first = received[source, 10]
        low = jnp.concatenate([first, first * (pairs[0][1] / pairs[0][0])], axis=0)
        up, mp, m, rp, r = (jnp.concatenate(pair, axis=0) for pair in pairs)
        return up, mp, low, m, [rp], [r]

    whole = tree(one, 0, received.shape[0], keep)
    for place, value in enumerate(listed(whole)):
        for target in range(sent.shape[0]):
            sent[target, pl.ds(4 * place, 4)] = value


def chain_back(received, kept, sent, bound):
    groups, chips = received.shape[0], sent.shape[0] // 2
    sources, targets = places(FAR_ORDER), places(BACK_ORDER)
    top = {}

    def keep(index, a, b, c):
        top[index] = a, b, c[0]

    def give(index, value):
        bound[index + 1] = value

    up, mp, low, m, rp, r = tree(lambda index: element_at(received, sources[index]), 0, groups, keep)
    zero = jnp.zeros_like(up)
    value = r[0] / (low + m)
    bound[0] = zero
    give(groups - 1, value)
    untree(lambda index: top[index], 0, groups, zero, value, give)
    mine = lax.axis_index("tun") // (2 * chips)
    before, value = bound[mine], bound[mine + 1]

    def end(index, value):
        for core in range(2):
            sent[targets[2 * index + core], 4:8] = value
            if index + 1 < chips:
                sent[targets[2 * index + 2 + core], 0:4] = value

    for core in range(2):
        sent[targets[core], 0:4] = before
    end(chips - 1, value)
    untree(lambda index: [kept[index, place] for place in range(3)], 0, chips, before, value, end)


def split(value):
    high = value.astype(jnp.bfloat16)
    return high, (value - high.astype(F32)).astype(jnp.bfloat16)


def tunnel_back(received, paired, kept, high, low, face, out, carried, solved, top_matrix, rest_matrix, done):
    @pl.when(early())
    def _():
        top_matrix[...], rest_matrix[...] = high[...], low[...]

    @pl.when(jnp.logical_not(early()))
    def _():
        width_inverse(face, top_matrix, rest_matrix)

    sources = places(BACK_ORDER)
    first = lax.axis_index("tun") % 2 == 0
    for group in range(8):
        comp, block = group // 4, group % 4
        for half in range(2):
            lanes = pl.ds(half * LANES, LANES)
            parts = [sources[8 * block + 2 * part + half] for part in range(4)]
            before, value = (
                jnp.concatenate([received[part, pl.ds(start + 2 * comp, 2)] for part in parts], axis=0)
                for start in (0, 4)
            )
            a, b, c = (paired[group, half, place] for place in range(3))
            centre = c + a * before + b * value
            before, value = jnp.where(first, before, centre), jnp.where(first, centre, value)
            for index in range(3, -1, -1):
                if index < 3:
                    a, b, c = (kept[group, index, place, :, lanes] for place in range(3))
                    value = c + a * before + b * value
                carried[pl.ds(128 * comp + 32 * index + 8 * block, 8), lanes] = value

    def times(one, two):
        return jnp.dot(one, two[...], preferred_element_type=F32)

    top, rest = split(carried[...])
    both = times(jnp.concatenate([top, rest], axis=0), top_matrix)
    solved[...] = both[:256] + (times(top, rest_matrix) + both[256:])
    copies = []
    for part in range(4):
        rows = pl.ds(64 * part, 64)
        copy = pltpu.make_async_copy(solved.at[rows, :], out.at[rows, :], done.at[part])
        copy.start()
        copies.append(copy)
    for copy in copies:
        copy.wait()


def width_inverse(face, high, low_part):
    count = 256
    step = 1

    def filled(start):
        parts = [face[start + LANES * half : start + LANES * (half + 1)] for half in range(2)]
        return jnp.concatenate([jnp.transpose(jnp.broadcast_to(part.reshape(1, LANES), (LANES, LANES))) for part in parts], axis=0)

    lower, upper = filled(0), filled(1)
    row = lax.broadcasted_iota(jnp.int32, (count, LANES), 0)
    one = jnp.ones((count, LANES), F32)
    m = one + jnp.where(row == 0, lower, 0.0) + jnp.where(row == count - 1, upper, 0.0)
    low, up = jnp.where(row == 0, 0.0, lower), jnp.where(row == count - 1, 0.0, upper)
    column = lax.broadcasted_iota(jnp.int32, (count, LANES), 1)
    rights = [jnp.where(row == column + LANES * half, 1.0, 0.0) for half in range(2)]

    def earlier(value, step):
        return jnp.concatenate([jnp.zeros_like(value[:step]), value[:-step]], axis=0)

    def later(value, step):
        return jnp.concatenate([value[step:], jnp.zeros_like(value[:step])], axis=0)

    while step < count:
        inverse = 1.0 / (low + m + up)
        part = m * inverse
        scaled = [right * inverse for right in rights]
        rights = [
            right + low * earlier(value, step) + up * later(value, step) for right, value in zip(rights, scaled)
        ]
        m, low, up = (
            m + low * earlier(part, step) + up * later(part, step),
            low * earlier(low * inverse, step),
            up * later(up * inverse, step),
        )
        step *= 2
    for half in range(2):
        lanes = pl.ds(half * LANES, LANES)
        top, rest = split(rights[half] / m)
        high[:, lanes] = top
        low_part[:, lanes] = rest


def call(kernel, outs, scratch, *args, place=pltpu.VMEM, out_place=pltpu.VMEM):
    if place is pltpu.HBM:
        args = [pltpu.with_memory_space_constraint(arg, place) for arg in args]
    return pl.pallas_call(
        kernel,
        out_shape=[jax.ShapeDtypeStruct(shape, dtype) for shape, dtype in outs],
        in_specs=[pl.BlockSpec(memory_space=place)] * len(args),
        out_specs=[pl.BlockSpec(memory_space=out_place)] * len(outs),
        scratch_shapes=scratch,
        compiler_params=pltpu.CompilerParams(vmem_limit_bytes=16 * 2**20),
    )(*args)


def room(*shape):
    return pltpu.VMEM(shape, F32)


def per_device(cotangent, tun_cond, tun_flow, heat_loss, hgt_cond, hgt_lift, wid_cond):
    chips, members = len(JOIN_ORDER), len(BACK_ORDER)
    count = lax.axis_size("tun")
    cores = [[first, first + 1] for first in range(0, count, 2)]
    join = [[first + 2 * chip + core for chip in JOIN_ORDER] for first in range(0, count, members) for core in range(2)]
    back = [[first + member for member in BACK_ORDER] for first in range(0, count, members)]
    far = [[first + members * group for group in FAR_ORDER] for first in range(members)]
    groups = len(FAR_ORDER)

    def exchanged(value, axis, groups=None):
        return lax.all_to_all(value, axis, 0, 0, tiled=True, axis_index_groups=groups)

    def rows(value):
        return value.reshape(-1, 256)

    elements, saved, middle, high, low, face = call(
        front,
        [((4, 32, 256), F32), ((4, 15, 8, 256), F32), ((16, 256), F32), *[((256, 256), jnp.bfloat16)] * 2, ((257,), F32)],
        [
            room(2, 8, 8, LANES),
            room(2, 256, LANES),
            room(2, 128, LANES),
            room(2, 128, LANES),
            pltpu.SemaphoreType.DMA((7,)),
        ],
        rows(cotangent),
        rows(hgt_cond),
        rows(hgt_lift),
        wid_cond,
        place=pltpu.HBM,
    )
    elements = exchanged(elements, "hgt", [list(HEIGHT_ORDER)])
    sent, kept = call(
        height_back,
        [((8, 2, 6, 8, LANES), F32), ((8, 3, 3, 8, 256), F32)],
        [room(5, 8, 256), room(2, 2, 2, 8, LANES), room(2, 256, LANES)],
        elements,
        saved,
        middle,
        rows(tun_cond),
        rows(tun_flow),
        rows(heat_loss),
    )
    received = lax.all_gather(sent, "tun", axis_index_groups=cores)
    sent, paired = call(
        pair_forward, [((chips, 11, 2, LANES), F32), ((8, 2, 3, 8, LANES), F32)], [], received
    )
    received = exchanged(sent, "tun", join)
    sent, chain = call(
        chain_forward, [((groups, 24, LANES), F32), ((chips - 1, 3, 4, LANES), F32)], [], received
    )
    received = exchanged(sent, "tun", far)
    [sent] = call(chain_back, [((members, 8, LANES), F32)], [room(groups + 1, 4, LANES)], received, chain)
    received = exchanged(sent, "tun", back)
    [solved] = call(
        tunnel_back,
        [((256, 256), F32)],
        [
            room(256, 256),
            room(256, 256),
            pltpu.VMEM((256, 256), jnp.bfloat16),
            pltpu.VMEM((256, 256), jnp.bfloat16),
            pltpu.SemaphoreType.DMA((4,)),
        ],
        received,
        paired,
        kept,
        high,
        low,
        face,
        out_place=pltpu.HBM,
    )
    return solved.reshape(cotangent.shape)


def solution(mesh):
    in_specs = (
        P(None, "tun", "hgt", None),
        P("tun", "hgt", None),
        P("tun", "hgt", None),
        P("tun", "hgt", None),
        P("tun", "hgt", None),
        P("tun", "hgt", None),
        P(),
    )
    out_specs = P(None, "tun", "hgt", None)
    return jax.shard_map(
        per_device, mesh=mesh, in_specs=in_specs, out_specs=out_specs, check_vma=False
    )
```
